128 devices in a mesh: tm: 32 (over x, z_lo, y), fsdp: 4 (over z_hi, core).
Axes of the slice: x: 4, y: 4, z: 4 (z_hi: 2, z_lo: 2; z = z_hi * 2 + z_lo), core: 2. Of those that a mesh axis runs over, the one named last changes fastest.
Arguments:
- latents: bfloat16 [24576, 4096], P('tm'), may hold values from -64 to 64
- out_grads: bfloat16 [24576, 8192], P('tm', 'fsdp'), may hold values from -0.64 to 0.64
- eig_in: float32 [8, 512, 512], replicated, may hold values from -0.25 to 0.25
- eig_out: float32 [16, 512, 512], P('fsdp'), may hold values from -0.25 to 0.25
- owner_table: int32 [32], replicated, may hold values from 0 to 31, each once
Outputs:
- update: float32 [4, 32, 512, 512], P(None, 'tm')
The draws below stay inside these ranges and needn't reach their ends.
Inputs may be any that keep to these rules, and one draw needn't show every extreme that they name: `owner_table`: every block number 0 to 31 stands exactly once.
All inputs are finite; a program needn't handle non-finite values.
Results may differ from the reference program's by a relative error of at most 0.0003.
Values sent between devices are 32-bit elements; how exact they have to be, the bound alone decides.
No kernel may reach another device: no remote copies, remote signals or barrier semaphores. Data moves between devices by JAX's collectives and lax.ppermute only.
A program may use at most 256 MiB of HBM per device.

```python
import math
import jax
import jax.numpy as jnp
from jax import lax

BLK = 512
DW = 4096
FFW = 8192
TOK_DEV = 768
TOKENS = 24576
NBA = 8
NBG = 32
N_TM = 32
N_FSDP = 4


def draw_latents(key, part):
    key = jax.random.fold_in(key, 11)
    first, second, third = jax.random.split(key, 3)
    core = jnp.clip(jax.random.normal(first, (TOKENS, DW), jnp.float32), -5.0, 5.0)
    columns = jnp.exp(jax.random.uniform(second, (1, DW), jnp.float32, math.log(0.3), math.log(3.0)))
    rows = jnp.exp(jax.random.uniform(third, (TOKENS, 1), jnp.float32, math.log(0.4), math.log(4.0)))
    return (core * columns * rows).astype(jnp.bfloat16)


def draw_out_grads(key, part):
    key = jax.random.fold_in(key, 23)
    first, second, third = jax.random.split(key, 3)
    core = jnp.clip(jax.random.normal(first, (TOKENS, FFW), jnp.float32), -5.0, 5.0)
    columns = jnp.exp(jax.random.uniform(second, (1, FFW), jnp.float32, math.log(0.3), math.log(3.0)))
    rows = jnp.exp(jax.random.uniform(third, (TOKENS, 1), jnp.float32, math.log(0.4), math.log(4.0)))
    return (0.01 * core * columns * rows).astype(jnp.bfloat16)


def steps_of(stream_key, extent, shards, least, top_value):
    def one(axis_at, blocks):
        draws = jax.random.uniform(jax.random.fold_in(jax.random.fold_in(stream_key, 6), axis_at), (blocks,), jnp.float32, least / len(shards), top_value / len(shards))
        return jnp.repeat(jnp.exp(draws), extent[axis_at] // blocks).reshape((-1,) + (1,) * (len(extent) - axis_at - 1))

    gain = one(*shards[0])
    for cut in shards[1:]:
        gain = gain * one(*cut)
    return gain


def bell_draw(key, shape, scale, reach, shards=(), kind=jnp.bfloat16):
    result = scale * jax.random.normal(key, shape, jnp.float32)
    if shards:
        result = result * steps_of(key, shape, shards, -0.22, 0.18)
    return jnp.clip(result, -reach, reach).astype(kind)


def setup_inputs(seed: int = 0) -> dict:
    arg_keys = jax.random.split(jax.random.key(seed), 6)
    latents = draw_latents(jax.random.fold_in(arg_keys[5], 71), 0)
    out_grads = draw_out_grads(jax.random.fold_in(arg_keys[5], 71), 0)
    eig_in = bell_draw(arg_keys[2], (NBA, BLK, BLK), BLK ** -0.5, 0.25, (), jnp.float32)
    eig_out = bell_draw(arg_keys[3], (FFW // BLK, BLK, BLK), BLK ** -0.5, 0.25, ((0, 4),), jnp.float32)
    owner_table = jax.random.permutation(arg_keys[4], NBG).astype(jnp.int32)
    return dict(latents=latents, out_grads=out_grads, eig_in=eig_in, eig_out=eig_out, owner_table=owner_table)


DAMPING = 0.0001
HIGH_ACCURACY = lax.Precision.HIGHEST


def diag_rotated(basis, factor):
    moved = jnp.einsum('abc,ack->abk', factor, basis, precision=HIGH_ACCURACY)
    return jnp.sum(basis * moved, axis=1)


def reference(latents, out_grads, eig_in, eig_out, owner_table):
    in_blocks = DW // BLK
    all_cols = FFW // BLK
    col_blocks = FFW // (BLK * N_FSDP)
    slots = in_blocks * col_blocks
    tokens_all = TOK_DEV * N_TM
    groups_in = latents.reshape(N_TM, TOK_DEV, DW)
    groups_out = out_grads.reshape(N_TM, TOK_DEV, FFW)

    def accumulate(carry, pair):
        grad_sum, input_factor_matrix, output_factor_matrix = carry
        x_rows = pair[0].astype(jnp.float32)
        y_rows = pair[1].astype(jnp.float32)
        partial_value = jnp.dot(x_rows.T, y_rows, preferred_element_type=jnp.float32, precision=HIGH_ACCURACY)
        input_rows_partitioned = x_rows.reshape(TOK_DEV, in_blocks, BLK)
        output_rows_partitioned = y_rows.reshape(TOK_DEV, all_cols, BLK)
        input_factor_matrix = input_factor_matrix + jnp.einsum('qhl,qhv->hlv', input_rows_partitioned, input_rows_partitioned, precision=HIGH_ACCURACY)
        output_factor_matrix = output_factor_matrix + jnp.einsum('qhl,qhv->hlv', output_rows_partitioned, output_rows_partitioned, precision=HIGH_ACCURACY)
        return (grad_sum + partial_value, input_factor_matrix, output_factor_matrix), None

    start = (jnp.zeros((DW, FFW), jnp.float32), jnp.zeros((in_blocks, BLK, BLK), jnp.float32), jnp.zeros((all_cols, BLK, BLK), jnp.float32))
    (grad_sum, input_factor_matrix, output_factor_matrix), _ = lax.scan(accumulate, start, (groups_in, groups_out))
    grad = grad_sum / tokens_all
    eigen_in = diag_rotated(eig_in, input_factor_matrix / tokens_all)
    eigen_out = diag_rotated(eig_out, output_factor_matrix / tokens_all)
    grad_blocks = grad.reshape(in_blocks, BLK, all_cols, BLK).transpose(0, 2, 1, 3)
    group_ids = jnp.arange(N_FSDP, dtype=jnp.int32)[:, None]
    row_ids = jnp.broadcast_to((owner_table // col_blocks)[None, :], (N_FSDP, slots)).reshape(-1)
    col_ids = (group_ids * col_blocks + (owner_table % col_blocks)[None, :]).reshape(-1)

    def precondition(pair):
        row_block, col_block = pair
        block = grad_blocks[row_block, col_block]
        basis_in = eig_in[row_block]
        basis_out = eig_out[col_block]
        rotated = jnp.dot(jnp.dot(basis_in.T, block, precision=HIGH_ACCURACY), basis_out, precision=HIGH_ACCURACY)
        scaled = rotated / (eigen_in[row_block][:, None] * eigen_out[col_block][None, :] + DAMPING)
        return jnp.dot(jnp.dot(basis_in, scaled, precision=HIGH_ACCURACY), basis_out.T, precision=HIGH_ACCURACY)

    update = lax.map(precondition, (row_ids.astype(jnp.int32), col_ids.astype(jnp.int32)))
    return update.reshape(N_FSDP, slots, BLK, BLK)
```

```python
import functools

import jax
import jax.numpy as jnp
from jax import lax
from jax.experimental import pallas as pl
from jax.experimental.pallas import tpu as pltpu
from jax.sharding import PartitionSpec as P

DAMPING = 0.0001
AXES = ("tm", "fsdp")
NX, NZ, NY = 4, 2, 4
N_TM, N_FSDP = 32, 4
BLK = 512
ROWS_A = 192
ROWS_C = (BLK - 2 * ROWS_A) // 2
EXTRA = 8
SMALL, LARGE = 16 * 1024 * 1024, 56 * 1024 * 1024


def flat(x, zl, y, zh, core):
    return ((x % NX) * 8 + zl * 4 + (y % NY)) * N_FSDP + zh * 2 + core


def coords():
    for x in range(NX):
        for zl in range(NZ):
            for y in range(NY):
                for zh in range(2):
                    for core in range(2):
                        yield x, zl, y, zh, core


def pairs_far(axis, d):
    return [
        (flat(x, zl, y, zh, c), flat(x + d * (axis == "x"), zl, y + d * (axis == "y"), zh, c))
        for x, zl, y, zh, c in coords()
    ]


def pairs_z(step):
    out = []
    for x, zl, y, zh, c in coords():
        z = (zh * 2 + zl + (step if zl == 0 else -step)) % 4
        out.append((flat(x, zl, y, zh, c), flat(x, z % 2, y, z // 2, c)))
    return out


def pairs_core():
    return [
        (flat(x, zl, y, zh, c), flat(x, zl, y, zh, 1 - c))
        for x, zl, y, zh, c in coords()
    ]


def split(value):
    high = value.astype(jnp.bfloat16)
    low = (value - high.astype(jnp.float32)).astype(jnp.bfloat16)
    return high, low


def dot3(a, b, dims):
    (ah, al), (bh, bl) = a, b
    dot = functools.partial(
        lax.dot_general,
        dimension_numbers=(dims, ((), ())),
        preferred_element_type=jnp.float32,
    )
    return dot(ah, bh) + (dot(ah, bl) + dot(al, bh))


def spot(where, stream, r, sub, i):
    z = where[1] if sub == 0 else 1 - where[1]
    if stream == "x":
        return ((where[0] + r) & 3) * 8 + z * 4 + i
    if stream == "y":
        return i * 8 + z * 4 + ((where[2] + r) & 3)
    return (i >> 2) * 8 + z * 4 + (i & 3)


def spec(shape, index, **more):
    return pl.BlockSpec(shape, index, **more)


def resident(array):
    zeros = (0,) * array.ndim
    return pl.BlockSpec(array.shape, lambda *_: zeros, pipeline_mode=pl.Buffered(1))


class Order:
    def __init__(self, table, where):
        self.table, self.where, self.last = table, where, None

    def gate(self, held, behind):
        anywhere = pl.BlockSpec(memory_space=pl.ANY)
        made = pl.pallas_call(
            lambda *refs: None,
            out_shape=[jax.ShapeDtypeStruct(a.shape, a.dtype) for a in held],
            in_specs=[anywhere] * (len(held) + len(behind) + 1),
            out_specs=[anywhere] * len(held),
            input_output_aliases={i: i for i in range(len(held))},
            cost_estimate=pl.CostEstimate(flops=0, bytes_accessed=1, transcendentals=0),
        )(*held, *behind, self.last)
        self.last = made[-1]
        return made

    def __call__(self, body, grid, ins, outs, cost=1.0, vmem=SMALL):
        shapes = [
            jax.ShapeDtypeStruct(o[0], o[2] if len(o) > 2 else jnp.float32) for o in outs
        ]
        inner = body
        if self.last is not None:
            ins = [(self.last, pl.BlockSpec(memory_space=pl.ANY))] + ins
            inner = lambda table, where, after, *refs: body(table, where, *refs)
        made = pl.pallas_call(
            inner,
            out_shape=shapes,
            grid_spec=pltpu.PrefetchScalarGridSpec(
                num_scalar_prefetch=2,
                grid=(grid,),
                in_specs=[s for _, s in ins],
                out_specs=[o[1] for o in outs],
            ),
            cost_estimate=pl.CostEstimate(
                flops=0, bytes_accessed=int(cost * 3.69e6), transcendentals=0
            ),
            compiler_params=pltpu.CompilerParams(vmem_limit_bytes=vmem),
        )(self.table, self.where, *[a for a, _ in ins])
        self.last = made[-1]
        return made


def piece(turned, latents, block, row, rows):
    left = turned[pl.ds(pl.multiple_of((block & 3) * BLK + row, 16), rows), :]
    right = latents[:, pl.ds(pl.multiple_of((block >> 2) * BLK, BLK), BLK)]
    return jnp.dot(left, right, preferred_element_type=jnp.float32)


SETS_A = (("x", 0, 2), ("x", 1, 2), ("y", 0, 2), ("y", 1, 2))
SETS_B = (("x", 1, 1), ("x", 0, 3), ("y", 1, 1), ("y", 0, 3))
SETS_T = (("x", 0, 1), ("x", 1, 3), ("y", 0, 1), ("y", 1, 3))
SETS_OWN = (("x", 0, 0), ("x", 1, 0), ("y", 0, 0), ("y", 1, 0))
SETS_AWAY, SETS_KEEP = (("c", 0, 0),), (("c", 1, 0),)
ROW = {"x": 0, "y": ROWS_A, "c": 2 * ROWS_A}


def first_body(table, where, grads, *refs):
    rights, turned, outs = refs[:4], refs[4], refs[5:]
    i = pl.program_id(0)

    @pl.when(i == 0)
    def _():
        for c in range(grads.shape[1] // BLK):
            turned[c * BLK : (c + 1) * BLK, :] = grads[:, c * BLK : (c + 1) * BLK].T

    for right, out, (stream, sub, r) in zip(rights, outs, SETS_A):
        block = table[spot(where, stream, r, sub, i)]
        row = (block & 3) * BLK + ROW[stream]
        left = turned[pl.ds(pl.multiple_of(row, 16), ROWS_A), :]
        out[0] = jnp.dot(left, right[...], preferred_element_type=jnp.float32)


def first_products(order, latents, out_grads):
    tok, wide = out_grads.shape
    ins = [(out_grads, resident(out_grads))]
    for job in SETS_A:
        at = lambda i, t, w, job=job: (0, t[spot(w, job[0], job[2], job[1], i)] >> 2)
        ins.append((latents, spec((tok, BLK), at)))
    outs = [((wide, tok), spec((wide, tok), lambda i, t, w: (0, 0)), out_grads.dtype)]
    for _ in SETS_A:
        outs.append(((4, ROWS_A, BLK), spec((1, ROWS_A, BLK), lambda i, t, w: (i, 0, 0))))
    return order(first_body, 4, ins, outs, vmem=LARGE)


def products_body(jobs, table, where, turned, latents, *refs):
    outs, got = refs[-len(jobs) :], refs[: -len(jobs)]
    i = pl.program_id(0)
    for m, ((stream, sub, r), out) in enumerate(zip(jobs, outs)):
        n, rows = out.shape[:2]
        for u in range(n):
            at = spot(where, stream, r, sub, n * i + u)
            value = piece(turned, latents, table[at], ROW[stream], rows)
            if m < len(got):
                value = value + got[m][u]
            out[u] = value


def products(order, turned, latents, jobs, got=()):
    outs = []
    for stream, sub, r in jobs:
        n, rows = (4, ROWS_A) if stream in "xy" else (16, 2 * ROWS_C)
        outs.append(((n, rows, BLK), spec((n // 4, rows, BLK), lambda i, t, w: (i, 0, 0))))
    return order(
        functools.partial(products_body, jobs),
        4,
        [(turned, resident(turned)), (latents, resident(latents))]
        + [(g, spec((1, ROWS_A, BLK), lambda i, t, w: (i, 0, 0))) for g in got],
        outs,
        vmem=LARGE,
    )


def whole(array):
    zeros = (0,) * array.ndim
    return spec(array.shape, lambda i, t, w: zeros)


def full(*shape):
    zeros = (0,) * len(shape)
    return (shape, spec(shape, lambda i, t, w: zeros))


def relay_body(table, where, *refs):
    for got, term, out in zip(refs[:4], refs[4:8], refs[8:]):
        out[...] = got[...] + term[...]


def relay(order, got, terms):
    here = spec((1, ROWS_A, BLK), lambda i, t, w: (i, 0, 0))
    ins = [(a, here) for a in (*got, *terms)]
    return order(relay_body, 4, ins, [(got[0].shape, here)] * 4, vmem=LARGE)


def half_rows(stream):
    return ROWS_A + 2 * (ROWS_C + (EXTRA if stream == "x" else 0))


MESSAGES = ((2, 0, (0, 0)), (1, 1, (0, 1)), (2, 1, (1, 0)), (3, 0, (1, 1)))
TERMS = ((1, 0, (0,)), (3, 1, (1,)), (0, 0, (2, 0)), (0, 1, (2, 1)))


def turn_body(stream, jobs, table, where, *refs):
    sums = refs[16:19] if stream == "x" else ()
    outs = refs[16 + len(sums) :]
    rows = (half_rows(stream) - ROWS_A) // 2
    for n, (r, half, place) in enumerate(jobs):
        base, more, got, term = refs[4 * n : 4 * n + 4]
        out = outs[place[0]].at[place[1]] if len(place) == 2 else outs[place[0]]
        out[:ROWS_A, :] = base[0] + more[0]
        for v in range(2):
            at = (0, v) if stream == "y" else (v, 0)
            low = ROWS_A + v * rows
            out[low : low + ROWS_C, :] = got[at] + term[at]
            if stream == "y":
                continue
            first_in, second_in, sums_out = sums
            parts = []
            for sub in (1, 0):
                block = table[spot(where, "y", r, sub, 2 * half + v)]
                a = block >> 2
                parts.append(jnp.where(a < 4, first_in[a & 3], second_in[a & 3]))
                parts.append(sums_out[block & 3])
            parts.append(jnp.zeros((EXTRA - 4, BLK), jnp.float32))
            out[low + ROWS_C : low + rows, :] = jnp.concatenate(parts, axis=0)


def turn(order, stream, jobs, halves, got, terms, sums):
    ins = []
    for r, half, _ in jobs:
        if stream == "x":
            here = lambda i, t, w, r=r: ((w[2] + r) & 3, 0, 0)
            side = spec((2, 1, ROWS_C, BLK), lambda i, t, w, r=r, h=half: (h, (w[2] + r) & 3, 1, 0))
        else:
            here = lambda i, t, w, r=r: ((w[0] + r) & 3, 0, 0)
            side = spec((1, 2, ROWS_C, BLK), lambda i, t, w, r=r, h=half: ((w[0] + r) & 3, h, 0, 0))
        ins += [(a, spec((1, ROWS_A, BLK), here)) for a in halves[half]]
        ins += [(a.reshape(4, 4, 2 * ROWS_C, BLK), side) for a in (got, terms)]
    if stream == "x":
        ins += [(s, whole(s)) for s in sums]
    rows = half_rows(stream)
    outs = [full(2, rows, BLK)] * 2
    if jobs is TERMS:
        outs = [full(rows, BLK)] * 2 + [full(2, rows, BLK)]
    return order(functools.partial(turn_body, stream, jobs), 1, ins, outs, vmem=LARGE)


def relay_half_body(table, where, message, term, out):
    out[...] = message[0] + term[...]


def relay_half(order, message, term):
    rows = message.shape[1]
    ins = [(message, spec((1, rows, BLK), lambda i, t, w: (0, 0, 0))), (term, whole(term))]
    return order(relay_half_body, 1, ins, [full(rows, BLK)])[0]


def end_body(stream, table, where, own, forth, back, more_forth, more_back, *outs):
    halves = (
        lambda a, b: own[0, a:b] + back[1, a:b] + more_forth[a:b, :],
        lambda a, b: own[1, a:b] + forth[1, a:b] + more_back[a:b, :],
    )
    outs[0][...] = halves[0](0, ROWS_A)
    outs[1][...] = halves[1](0, ROWS_A)
    rows = (half_rows(stream) - ROWS_A) // 2
    for u in range(4):
        base = ROWS_A + (u % 2) * rows
        slot = halves[u // 2](base, base + rows)
        for d in range(4):

            @pl.when(((where[0 if stream == "x" else 2] + d) & 3) == u)
            def _():
                outs[2 + d][...] = slot


def end(order, stream, own, forth, back, more_forth, more_back):
    rows = (half_rows(stream) - ROWS_A) // 2
    outs = [full(ROWS_A, BLK)] * 2 + [full(rows, BLK)] * 4
    ins = [(a, whole(a)) for a in (own, forth, back, more_forth, more_back)]
    return order(functools.partial(end_body, stream), 1, ins, outs)


def sums_body(table, where, rows, basis, out):
    high, low = split(basis[0])
    tokens = rows[...]
    moved = jnp.dot(
        jnp.concatenate([tokens, tokens], axis=1),
        jnp.concatenate([high, low], axis=0),
        preferred_element_type=jnp.float32,
    )
    out[0] = jnp.sum(moved * moved, axis=0, keepdims=True)


def square_sums(order, rows, basis, first, n):
    tok = rows.shape[0]
    ins = [
        (rows, spec((tok, BLK), lambda i, t, w: (0, first + i))),
        (basis, spec((1, BLK, BLK), lambda i, t, w: (first + i, 0, 0))),
    ]
    out = ((n, 1, BLK), spec((1, 1, BLK), lambda i, t, w: (i, 0, 0)))
    return order(sums_body, n, ins, [out], vmem=LARGE)[0]


def total_body(table, where, *refs):
    value = (refs[0][...] + refs[1][...]) + (refs[2][...] + refs[3][...])
    refs[4][...] = value[:ROWS_C]
    if len(refs) == 6:
        refs[5][...] = value[ROWS_C:]


def total(order, parts):
    rows = parts[0].shape[0]
    outs = [full(ROWS_C, BLK)] + ([full(EXTRA, BLK)] if rows > ROWS_C else [])
    return order(total_body, 1, [(p, whole(p)) for p in parts], outs)


def join_body(table, where, a, b, out):
    out[...] = a[...] + b[...]


def join(order, a, b):
    return order(join_body, 1, [(a, whole(a)), (b, whole(b))], [full(*a.shape)])[0]


def precondition_body(tokens_all, table, where, *refs):
    x, y0, y1, cx, cy, ours, theirs = (r[...] for r in refs[:7])
    basis_in, basis_out, out = refs[7:]
    scale = 1.0 / tokens_all
    grad = jnp.concatenate([x, y0 + y1, cx, cy], axis=0) * scale
    values_in = (ours[0:1] + theirs[2:3]) * scale
    values_out = (ours[1:2] + theirs[3:4]) * scale
    a = split(basis_in[0])
    b = split(basis_out[0])
    rotated = dot3(split(grad), a, ((1,), (0,)))
    rotated = dot3(b, split(rotated), ((0,), (0,)))
    scaled = rotated / (values_out.reshape(BLK, 1) * values_in + DAMPING)
    back = dot3(b, split(scaled), ((1,), (0,)))
    out[...] = dot3(a, split(back), ((1,), (1,)))


def precondition(tokens_all, order, parts, eig_in, eig_out):
    mine = lambda w: w[0] * 8 + (1 - w[1]) * 4 + w[2]
    ins = [(q, whole(q)) for q in parts]
    ins.append((eig_in, spec((1, BLK, BLK), lambda i, t, w: (t[mine(w)] >> 2, 0, 0))))
    ins.append((eig_out, spec((1, BLK, BLK), lambda i, t, w: (t[mine(w)] & 3, 0, 0))))
    return order(
        functools.partial(precondition_body, tokens_all),
        1,
        ins,
        [full(BLK, BLK)],
        cost=3.0,
        vmem=LARGE,
    )[0]


def on_device(latents, out_grads, eig_in, eig_out, table):
    tokens_all = latents.shape[0] * N_TM
    tm = lax.axis_index("tm")
    fsdp = lax.axis_index("fsdp")
    x, zl, y = tm // 8, (tm // 4) % 2, tm % 4
    zh, core = fsdp // 2, fsdp % 2
    where = jnp.stack([x, zl, y]).astype(jnp.int32)
    near, cross = pairs_z(1), pairs_z(-1)
    send = lambda value, pairs: lax.ppermute(value, AXES, pairs)
    hop = lambda value, axis, d: send(value, pairs_far(axis, d))
    both = lambda forth, back, axis: [hop(forth, axis, 1), hop(back, axis, 3)]
    order = Order(table, where)
    far = lambda parts, axis: [parts[0]] + [hop(parts[d], axis, d) for d in (1, 2, 3)]

    turned, *sets_a = first_products(order, latents, out_grads)
    got_a = both(*sets_a[:2], "x") + both(*sets_a[2:], "y")
    got_c = send(products(order, turned, latents, SETS_AWAY)[0], near)
    made = products(order, turned, latents, SETS_B + SETS_T)
    got_b = both(*made[:2], "x") + both(*made[2:4], "y")
    sets_t = relay(order, got_a, made[4:])
    sums = [square_sums(order, latents, eig_in, 0, 4)]
    got_t = both(*order.gate(sets_t[:2], got_b[:2]), "x")
    got_t += both(*order.gate(sets_t[2:], got_b[2:]), "y")
    got_b = [got_b[n] for n in (1, 0, 3, 2)]
    *own, terms_c = products(order, turned, latents, SETS_OWN + SETS_KEEP, got_b)
    sums.append(square_sums(order, latents, eig_in, 4, 4))
    sums.append(square_sums(order, out_grads, eig_out, 0, 4))

    def pieces(stream, jobs):
        n = 0 if stream == "x" else 2
        halves = ((own[n], got_t[n]), (own[n + 1], got_t[n + 1]))
        return turn(order, stream, jobs, halves, got_c, terms_c, sums)

    msgs_x = both(*pieces("x", MESSAGES), "y")
    msgs_y = both(*pieces("y", MESSAGES), "x")
    *parts_x, mine_x = pieces("x", TERMS)
    *parts_y, mine_y = pieces("y", TERMS)

    def follow(stream, messages, parts):
        more = [relay_half(order, m, p) for m, p in zip(messages, parts)]
        return both(*more, "y" if stream == "x" else "x")

    more_x = follow("x", msgs_x, parts_x)
    more_y = follow("y", msgs_y, parts_y)

    away_x, keep_x, *parts_cy = end(order, "x", mine_x, *msgs_x, *more_x)
    got_x = send(away_x, near)
    away_y, keep_y, *parts_cx = end(order, "y", mine_y, *msgs_y, *more_y)
    got_y = send(away_y, near)
    done_cy, ours = total(order, far(parts_cy, "x"))
    theirs = send(ours, near)
    (done_cx,) = total(order, far(parts_cx, "y"))
    done_x = join(order, keep_x, got_x)
    update = precondition(
        tokens_all,
        order,
        [done_x, keep_y, got_y, done_cx, done_cy, ours, theirs],
        eig_in,
        eig_out,
    )
    same = send(update, near)
    other = send(update, cross)
    same_core = send(same, pairs_core())
    other_core = send(other, pairs_core())
    result = jnp.zeros((N_FSDP, BLK, BLK), jnp.float32)
    for block, at in (
        (same, zh * 2 + core),
        (other, (1 - zh) * 2 + core),
        (same_core, zh * 2 + 1 - core),
        (other_core, (1 - zh) * 2 + 1 - core),
    ):
        result = lax.dynamic_update_index_in_dim(result, block, at, 0)
    return result[:, None]


def solution(mesh):
    in_specs = (P("tm", None), P("tm", "fsdp"), P(), P("fsdp", None, None), P())
    out_specs = P(None, "tm", None, None)
    return jax.shard_map(
        on_device, mesh=mesh, in_specs=in_specs, out_specs=out_specs, check_vma=False
    )
```

```python
import functools

import jax
import jax.numpy as jnp
from jax import lax
from jax.experimental import pallas as pl
from jax.experimental.pallas import tpu as pltpu
from jax.sharding import PartitionSpec as P

DAMPING = 0.0001
AXES = ("tm", "fsdp")
NX, NZ, NY = 4, 2, 4
N_TM, N_FSDP = 32, 4
BLK = 512
ROWS_A = 208
ROWS_C = BLK - 2 * ROWS_A
EXTRA = 8
SMALL, TURN, LARGE = 16 * 1024 * 1024, 30 * 1024 * 1024, 56 * 1024 * 1024


def flat(x, zl, y, zh, core):
    return ((x % NX) * 8 + zl * 4 + (y % NY)) * N_FSDP + zh * 2 + core


def coords():
    for x in range(NX):
        for zl in range(NZ):
            for y in range(NY):
                for zh in range(2):
                    for core in range(2):
                        yield x, zl, y, zh, core


def pairs_far(axis, d):
    return [
        (flat(x, zl, y, zh, c), flat(x + d * (axis == "x"), zl, y + d * (axis == "y"), zh, c))
        for x, zl, y, zh, c in coords()
    ]


def pairs_z(step):
    out = []
    for x, zl, y, zh, c in coords():
        z = (zh * 2 + zl + (step if zl == 0 else -step)) % 4
        out.append((flat(x, zl, y, zh, c), flat(x, z % 2, y, z // 2, c)))
    return out


def pairs_core():
    return [
        (flat(x, zl, y, zh, c), flat(x, zl, y, zh, 1 - c))
        for x, zl, y, zh, c in coords()
    ]


def split(value):
    high = value.astype(jnp.bfloat16)
    low = (value - high.astype(jnp.float32)).astype(jnp.bfloat16)
    return high, low


def dot3(a, b, dims):
    (ah, al), (bh, bl) = a, b
    dot = functools.partial(
        lax.dot_general,
        dimension_numbers=(dims, ((), ())),
        preferred_element_type=jnp.float32,
    )
    return dot(ah, bh) + (dot(ah, bl) + dot(al, bh))


def spot(where, stream, r, sub, i):
    z = where[1] if sub == 0 else 1 - where[1]
    if stream == "x":
        return ((where[0] + r) & 3) * 8 + z * 4 + i
    if stream == "y":
        return i * 8 + z * 4 + ((where[2] + r) & 3)
    return (i >> 2) * 8 + z * 4 + (i & 3)


def spec(shape, index, **more):
    return pl.BlockSpec(shape, index, **more)


def resident(array):
    zeros = (0,) * array.ndim
    return pl.BlockSpec(array.shape, lambda *_: zeros, pipeline_mode=pl.Buffered(1))


class Order:
    def __init__(self, table, where):
        self.table, self.where, self.last = table, where, None

    def gate(self, held, behind):
        anywhere = pl.BlockSpec(memory_space=pl.ANY)
        made = pl.pallas_call(
            lambda *refs: None,
            out_shape=[jax.ShapeDtypeStruct(a.shape, a.dtype) for a in held],
            in_specs=[anywhere] * (len(held) + len(behind) + 1),
            out_specs=[anywhere] * len(held),
            input_output_aliases={i: i for i in range(len(held))},
            cost_estimate=pl.CostEstimate(flops=0, bytes_accessed=1, transcendentals=0),
        )(*held, *behind, self.last)
        self.last = made[-1]
        return made

    def __call__(self, body, grid, ins, outs, cost=1.0, vmem=SMALL):
        shapes = [
            jax.ShapeDtypeStruct(o[0], o[2] if len(o) > 2 else jnp.float32) for o in outs
        ]
        inner = body
        if self.last is not None:
            ins = [(self.last, pl.BlockSpec(memory_space=pl.ANY))] + ins
            inner = lambda table, where, after, *refs: body(table, where, *refs)
        made = pl.pallas_call(
            inner,
            out_shape=shapes,
            grid_spec=pltpu.PrefetchScalarGridSpec(
                num_scalar_prefetch=2,
                grid=(grid,),
                in_specs=[s for _, s in ins],
                out_specs=[o[1] for o in outs],
            ),
            cost_estimate=pl.CostEstimate(
                flops=0, bytes_accessed=int(cost * 3.69e6), transcendentals=0
            ),
            compiler_params=pltpu.CompilerParams(vmem_limit_bytes=vmem),
        )(self.table, self.where, *[a for a, _ in ins])
        self.last = made[-1]
        return made


def piece(turned, latents, block, row, rows):
    left = turned[pl.ds(pl.multiple_of((block & 3) * BLK + row, 16), rows), :]
    right = latents[:, pl.ds(pl.multiple_of((block >> 2) * BLK, BLK), BLK)]
    return jnp.dot(left, right, preferred_element_type=jnp.float32)


SETS_A = (("x", 0, 2), ("x", 1, 2), ("y", 0, 2), ("y", 1, 2))
SETS_B = (("x", 1, 1), ("x", 0, 3), ("y", 1, 1), ("y", 0, 3))
SETS_T = (("x", 0, 1), ("x", 1, 3), ("y", 0, 1), ("y", 1, 3))
SETS_OWN = (("x", 0, 0), ("x", 1, 0), ("y", 0, 0), ("y", 1, 0))
SETS_AWAY, SETS_KEEP = (("c", 0, 0),), (("c", 1, 0),)
ROW = {"x": 0, "y": ROWS_A, "c": 2 * ROWS_A}


def first_body(table, where, grads, *refs):
    rights, turned, outs = refs[:4], refs[4], refs[5:]
    i = pl.program_id(0)

    @pl.when(i == 0)
    def _():
        for c in range(grads.shape[1] // BLK):
            turned[c * BLK : (c + 1) * BLK, :] = grads[:, c * BLK : (c + 1) * BLK].T

    for right, out, (stream, sub, r) in zip(rights, outs, SETS_A):
        block = table[spot(where, stream, r, sub, i)]
        row = (block & 3) * BLK + ROW[stream]
        left = turned[pl.ds(pl.multiple_of(row, 16), ROWS_A), :]
        out[0] = jnp.dot(left, right[...], preferred_element_type=jnp.float32)


def first_products(order, latents, out_grads):
    tok, wide = out_grads.shape
    ins = [(out_grads, resident(out_grads))]
    for job in SETS_A:
        at = lambda i, t, w, job=job: (0, t[spot(w, job[0], job[2], job[1], i)] >> 2)
        ins.append((latents, spec((tok, BLK), at)))
    outs = [((wide, tok), spec((wide, tok), lambda i, t, w: (0, 0)), out_grads.dtype)]
    for _ in SETS_A:
        outs.append(((4, ROWS_A, BLK), spec((1, ROWS_A, BLK), lambda i, t, w: (i, 0, 0))))
    return order(first_body, 4, ins, outs, vmem=LARGE)


def products_body(jobs, table, where, turned, latents, *refs):
    outs, got = refs[-len(jobs) :], refs[: -len(jobs)]
    i = pl.program_id(0)
    for m, ((stream, sub, r), out) in enumerate(zip(jobs, outs)):
        n, rows = out.shape[:2]
        for u in range(n):
            at = spot(where, stream, r, sub, n * i + u)
            value = piece(turned, latents, table[at], ROW[stream], rows)
            if m < len(got):
                value = value + got[m][u]
            out[u] = value


def products(order, turned, latents, jobs, got=()):
    outs = []
    for stream, sub, r in jobs:
        n, rows = (4, ROWS_A) if stream in "xy" else (16, ROWS_C)
        outs.append(((n, rows, BLK), spec((n // 4, rows, BLK), lambda i, t, w: (i, 0, 0))))
    return order(
        functools.partial(products_body, jobs),
        4,
        [(turned, resident(turned)), (latents, resident(latents))]
        + [(g, spec((1, ROWS_A, BLK), lambda i, t, w: (i, 0, 0))) for g in got],
        outs,
        vmem=LARGE,
    )


def whole(array):
    zeros = (0,) * array.ndim
    return spec(array.shape, lambda i, t, w: zeros)


def full(*shape):
    zeros = (0,) * len(shape)
    return (shape, spec(shape, lambda i, t, w: zeros))


def relay_body(table, where, *refs):
    for got, term, out in zip(refs[:4], refs[4:8], refs[8:]):
        out[...] = got[...] + term[...]


def relay(order, got, terms):
    here = spec((1, ROWS_A, BLK), lambda i, t, w: (i, 0, 0))
    ins = [(a, here) for a in (*got, *terms)]
    return order(relay_body, 4, ins, [(got[0].shape, here)] * 4, vmem=LARGE)


MESSAGES = ((2, 0, (0, 0)), (1, 1, (0, 1)), (2, 1, (1, 0)), (3, 0, (1, 1)))
TERMS = ((1, 0, (0,)), (3, 1, (1,)), (0, 0, (2, 0)), (0, 1, (2, 1)))


def turn_body(jobs, table, where, *refs):
    ins, outs = refs[: 2 * len(jobs)], refs[2 * len(jobs) :]
    for n, place in enumerate(jobs):
        out = outs[place[0]].at[place[1]] if len(place) == 2 else outs[place[0]]
        out[...] = ins[2 * n][0] + ins[2 * n + 1][0]


def turn(order, streams, pieces, halves):
    once = dict(pipeline_mode=pl.Buffered(1))
    ins, jobs, outs = [], [], []
    for stream in streams:
        at = 2 if stream == "x" else 0
        for r, half, place in pieces:
            jobs.append((place[0] + len(outs), *place[1:]))
            here = lambda i, t, w, at=at, r=r: ((w[at] + r) & 3, 0, 0)
            ins += [(a, spec((1, ROWS_A, BLK), here, **once)) for a in halves[stream][half]]
        if pieces is TERMS:
            outs += [full(ROWS_A, BLK)] * 2 + [full(2, ROWS_A, BLK)]
        else:
            outs += [full(2, ROWS_A, BLK)] * 2
    return order(functools.partial(turn_body, jobs), 1, ins, outs, vmem=TURN)


def relay_half_body(table, where, *refs):
    for message, term, out in zip(refs[:2], refs[2:4], refs[4:]):
        out[...] = message[0] + term[...]


def relay_half(order, messages, terms):
    half = spec((1, ROWS_A, BLK), lambda i, t, w: (0, 0, 0))
    ins = [(m, half) for m in messages] + [(a, whole(a)) for a in terms]
    return order(relay_half_body, 1, ins, [full(ROWS_A, BLK)] * 2, cost=1.0)


def end_body(table, where, own, forth, back, more_forth, more_back, away, keep):
    away[...] = own[0] + back[0] + more_forth[...]
    keep[...] = own[1] + forth[0] + more_back[...]


def end(order, own, forth, back, more_forth, more_back):
    half = spec((1, ROWS_A, BLK), lambda i, t, w: (1, 0, 0))
    ins = [(own, whole(own)), (forth, half), (back, half)]
    ins += [(a, whole(a)) for a in (more_forth, more_back)]
    return order(end_body, 1, ins, [full(ROWS_A, BLK)] * 2, cost=1.0)


def kept_body(table, where, got, term, ours, theirs, out):
    i = pl.program_id(0)
    for u in range(4):
        block = table[spot(where, "c", 0, 1, 4 * i + u)]
        a, c = block >> 2, 8 + (block & 3)
        out[u, :ROWS_C, :] = got[u] + term[u]
        out[u, ROWS_C:, :] = jnp.concatenate(
            [ours[a] + theirs[a], ours[c] + theirs[c], jnp.zeros((EXTRA - 2, BLK), jnp.float32)],
            axis=0,
        )


def kept(order, got, terms, ours, theirs):
    here = spec((4, ROWS_C, BLK), lambda i, t, w: (i, 0, 0))
    ins = [(got, here), (terms, here), (ours, whole(ours)), (theirs, whole(theirs))]
    rows = ROWS_C + EXTRA
    out = ((16, rows, BLK), spec((4, rows, BLK), lambda i, t, w: (i, 0, 0)))
    return order(kept_body, 4, ins, [out], vmem=TURN)[0]


def sums_body(table, where, rows, basis, out):
    high, low = split(basis[0])
    tokens = rows[...]
    moved = jnp.dot(
        jnp.concatenate([tokens, tokens], axis=1),
        jnp.concatenate([high, low], axis=0),
        preferred_element_type=jnp.float32,
    )
    out[0] = jnp.sum(moved * moved, axis=0, keepdims=True)


def square_sums(order, rows, basis, first, n):
    tok = rows.shape[0]
    ins = [
        (rows, spec((tok, BLK), lambda i, t, w: (0, first + i))),
        (basis, spec((1, BLK, BLK), lambda i, t, w: (first + i, 0, 0))),
    ]
    out = ((n, 1, BLK), spec((1, 1, BLK), lambda i, t, w: (i, 0, 0)))
    return order(sums_body, n, ins, [out], vmem=LARGE)[0]


def mine(w):
    return w[0] * 8 + (1 - w[1]) * 4 + w[2]


def rotate_body(table, where, first, second, basis, out):
    out[...] = dot3(split(first[...] + second[...]), split(basis[0]), ((1,), (0,)))


def rotate(order, first, second, eig_in):
    ins = [(a, whole(a)) for a in (first, second)]
    ins.append((eig_in, spec((1, BLK, BLK), lambda i, t, w: (t[mine(w)] >> 2, 0, 0))))
    return order(rotate_body, 1, ins, [full(*first.shape)], vmem=LARGE)[0]


def precondition_body(tokens_all, table, where, x, y0, y1, rest, basis_in, basis_out, out):
    scale = 1.0 / tokens_all
    sums = rest[0, ROWS_C:, :] * scale
    values_in, values_out = sums[0:1], sums[1:2]
    a = split(basis_in[0])
    b = split(basis_out[0])
    late = jnp.concatenate([y0[...] + y1[...], rest[0, :ROWS_C, :]], axis=0)
    rotated = jnp.concatenate([x[...], dot3(split(late), a, ((1,), (0,)))], axis=0) * scale
    rotated = dot3(b, split(rotated), ((0,), (0,)))
    scaled = rotated / (values_out.reshape(BLK, 1) * values_in + DAMPING)
    back = dot3(b, split(scaled), ((1,), (0,)))
    out[...] = dot3(a, split(back), ((1,), (1,)))


def precondition(tokens_all, order, parts, eig_in, eig_out):
    ins = [(q, whole(q)) for q in parts]
    ins.append((eig_in, spec((1, BLK, BLK), lambda i, t, w: (t[mine(w)] >> 2, 0, 0))))
    ins.append((eig_out, spec((1, BLK, BLK), lambda i, t, w: (t[mine(w)] & 3, 0, 0))))
    return order(
        functools.partial(precondition_body, tokens_all),
        1,
        ins,
        [full(BLK, BLK)],
        vmem=LARGE,
    )[0]


def on_device(latents, out_grads, eig_in, eig_out, table):
    tokens_all = latents.shape[0] * N_TM
    tm = lax.axis_index("tm")
    fsdp = lax.axis_index("fsdp")
    x, zl, y = tm // 8, (tm // 4) % 2, tm % 4
    zh, core = fsdp // 2, fsdp % 2
    where = jnp.stack([x, zl, y]).astype(jnp.int32)
    near, cross = pairs_z(1), pairs_z(-1)
    send = lambda value, pairs: lax.ppermute(value, AXES, pairs)
    hop = lambda value, axis, d: send(value, pairs_far(axis, d))
    both = lambda forth, back, axis: [hop(forth, axis, 1), hop(back, axis, 3)]
    order = Order(table, where)

    turned, *sets_a = first_products(order, latents, out_grads)
    got_a = both(*sets_a[:2], "x") + both(*sets_a[2:], "y")
    got_c = send(products(order, turned, latents, SETS_AWAY)[0], near)
    made = products(order, turned, latents, SETS_B + SETS_T)
    got_b = both(*made[:2], "x") + both(*made[2:4], "y")
    sets_t = relay(order, got_a, made[4:])
    sums = jnp.concatenate(
        [
            square_sums(order, latents, eig_in, 0, 4),
            square_sums(order, latents, eig_in, 4, 4),
            square_sums(order, out_grads, eig_out, 0, 4),
        ]
    )
    got_sums = send(sums, near)
    got_t = both(*order.gate(sets_t[:2], got_b[:2]), "x")
    got_t += both(*order.gate(sets_t[2:], got_b[2:]), "y")
    got_b = [got_b[n] for n in (1, 0, 3, 2)]
    *own, terms_c = products(order, turned, latents, SETS_OWN + SETS_KEEP, got_b)

    rest = kept(order, got_c, terms_c, sums, got_sums)
    planes = [[x * 8 + z * 4 + y for x in range(NX) for y in range(NY)] for z in range(NZ)]
    rest = lax.psum_scatter(rest, "tm", axis_index_groups=planes, tiled=True)
    halves = {
        stream: ((own[n], got_t[n]), (own[n + 1], got_t[n + 1]))
        for n, stream in ((0, "x"), (2, "y"))
    }
    messages = turn(order, "xy", MESSAGES, halves)
    msgs_x, msgs_y = both(*messages[:2], "y"), both(*messages[2:], "x")
    *parts_x, mine_x = turn(order, "x", TERMS, halves)
    *parts_y, mine_y = turn(order, "y", TERMS, halves)
    more_x = both(*relay_half(order, msgs_x, parts_x), "y")
    more_y = both(*relay_half(order, msgs_y, parts_y), "x")

    away_x, keep_x = end(order, mine_x, *msgs_x, *more_x)
    got_x = send(away_x, near)
    away_y, keep_y = end(order, mine_y, *msgs_y, *more_y)
    got_y = send(away_y, near)
    turned_x = rotate(order, keep_x, got_x, eig_in)
    update = precondition(
        tokens_all, order, [turned_x, keep_y, got_y, rest], eig_in, eig_out
    )
    same = send(update, near)
    other = send(update, cross)
    same_core = send(same, pairs_core())
    other_core = send(other, pairs_core())
    result = jnp.zeros((N_FSDP, BLK, BLK), jnp.float32)
    for block, at in (
        (same, zh * 2 + core),
        (other, (1 - zh) * 2 + core),
        (same_core, zh * 2 + 1 - core),
        (other_core, (1 - zh) * 2 + 1 - core),
    ):
        result = lax.dynamic_update_index_in_dim(result, block, at, 0)
    return result[:, None]


def solution(mesh):
    in_specs = (P("tm", None), P("tm", "fsdp"), P(), P("fsdp", None, None), P())
    out_specs = P(None, "tm", None, None)
    return jax.shard_map(
        on_device, mesh=mesh, in_specs=in_specs, out_specs=out_specs, check_vma=False
    )
```

```python
import functools

import jax
import jax.numpy as jnp
from jax import lax
from jax.experimental import pallas as pl
from jax.experimental.pallas import tpu as pltpu
from jax.sharding import PartitionSpec as P

DAMPING = 0.0001
AXES = ("tm", "fsdp")
NX, NZ, NY = 4, 2, 4
N_TM, N_FSDP = 32, 4
BLK = 512
ROWS_A = 192
ROWS_C = (BLK - 2 * ROWS_A) // 2
EXTRA = 8
SMALL, TURN, LARGE = 16 * 1024 * 1024, 30 * 1024 * 1024, 56 * 1024 * 1024


def flat(x, zl, y, zh, core):
    return ((x % NX) * 8 + zl * 4 + (y % NY)) * N_FSDP + zh * 2 + core


def coords():
    for x in range(NX):
        for zl in range(NZ):
            for y in range(NY):
                for zh in range(2):
                    for core in range(2):
                        yield x, zl, y, zh, core


def pairs_far(axis, d):
    return [
        (flat(x, zl, y, zh, c), flat(x + d * (axis == "x"), zl, y + d * (axis == "y"), zh, c))
        for x, zl, y, zh, c in coords()
    ]


def pairs_z(step):
    out = []
    for x, zl, y, zh, c in coords():
        z = (zh * 2 + zl + (step if zl == 0 else -step)) % 4
        out.append((flat(x, zl, y, zh, c), flat(x, z % 2, y, z // 2, c)))
    return out


def pairs_core():
    return [
        (flat(x, zl, y, zh, c), flat(x, zl, y, zh, 1 - c))
        for x, zl, y, zh, c in coords()
    ]


def split(value):
    high = value.astype(jnp.bfloat16)
    low = (value - high.astype(jnp.float32)).astype(jnp.bfloat16)
    return high, low


def dot3(a, b, dims):
    (ah, al), (bh, bl) = a, b
    dot = functools.partial(
        lax.dot_general,
        dimension_numbers=(dims, ((), ())),
        preferred_element_type=jnp.float32,
    )
    return dot(ah, bh) + (dot(ah, bl) + dot(al, bh))


def spot(where, stream, r, sub, i):
    z = where[1] if sub == 0 else 1 - where[1]
    if stream == "x":
        return ((where[0] + r) & 3) * 8 + z * 4 + i
    if stream == "y":
        return i * 8 + z * 4 + ((where[2] + r) & 3)
    return (i >> 2) * 8 + z * 4 + (i & 3)


def spec(shape, index, **more):
    return pl.BlockSpec(shape, index, **more)


def resident(array):
    zeros = (0,) * array.ndim
    return pl.BlockSpec(array.shape, lambda *_: zeros, pipeline_mode=pl.Buffered(1))


class Order:
    def __init__(self, table, where):
        self.table, self.where, self.last = table, where, None
        self.also = []

    def gate(self, held, behind):
        anywhere = pl.BlockSpec(memory_space=pl.ANY)
        made = pl.pallas_call(
            lambda *refs: None,
            out_shape=[jax.ShapeDtypeStruct(a.shape, a.dtype) for a in held],
            in_specs=[anywhere] * (len(held) + len(behind) + 1),
            out_specs=[anywhere] * len(held),
            input_output_aliases={i: i for i in range(len(held))},
            cost_estimate=pl.CostEstimate(flops=0, bytes_accessed=1, transcendentals=0),
        )(*held, *behind, self.last)
        self.last = made[-1]
        return made

    def __call__(self, body, grid, ins, outs, cost=1.0, vmem=SMALL):
        shapes = [
            jax.ShapeDtypeStruct(o[0], o[2] if len(o) > 2 else jnp.float32) for o in outs
        ]
        inner = body
        if self.last is not None:
            after = [self.last] + self.also
            self.also = []
            ins = [(a, pl.BlockSpec(memory_space=pl.ANY)) for a in after] + ins
            inner = lambda table, where, *refs: body(table, where, *refs[len(after) :])
        made = pl.pallas_call(
            inner,
            out_shape=shapes,
            grid_spec=pltpu.PrefetchScalarGridSpec(
                num_scalar_prefetch=2,
                grid=(grid,),
                in_specs=[s for _, s in ins],
                out_specs=[o[1] for o in outs],
            ),
            cost_estimate=pl.CostEstimate(
                flops=0, bytes_accessed=int(cost * 3.69e6), transcendentals=0
            ),
            compiler_params=pltpu.CompilerParams(vmem_limit_bytes=vmem),
        )(self.table, self.where, *[a for a, _ in ins])
        self.last = made[-1]
        return made


def piece(turned, latents, block, row, rows):
    left = turned[pl.ds(pl.multiple_of((block & 3) * BLK + row, 16), rows), :]
    right = latents[:, pl.ds(pl.multiple_of((block >> 2) * BLK, BLK), BLK)]
    return jnp.dot(left, right, preferred_element_type=jnp.float32)


SETS_A = (("x", 0, 2), ("x", 1, 2), ("y", 0, 2), ("y", 1, 2))
SETS_B = (("x", 1, 1), ("x", 0, 3), ("y", 1, 1), ("y", 0, 3))
SETS_T = (("x", 0, 1), ("x", 1, 3), ("y", 0, 1), ("y", 1, 3))
SETS_OWN = (("x", 0, 0), ("x", 1, 0), ("y", 0, 0), ("y", 1, 0))
SETS_AWAY, SETS_KEEP = (("c", 0, 0),), (("c", 1, 0),)
ROW = {"x": 0, "y": ROWS_A, "c": 2 * ROWS_A}


def first_body(table, where, grads, *refs):
    rights, turned, outs = refs[:4], refs[4], refs[5:]
    i = pl.program_id(0)

    @pl.when(i == 0)
    def _():
        for c in range(grads.shape[1] // BLK):
            turned[c * BLK : (c + 1) * BLK, :] = grads[:, c * BLK : (c + 1) * BLK].T

    for right, out, (stream, sub, r) in zip(rights, outs, SETS_A):
        block = table[spot(where, stream, r, sub, i)]
        row = (block & 3) * BLK + ROW[stream]
        left = turned[pl.ds(pl.multiple_of(row, 16), ROWS_A), :]
        out[0] = jnp.dot(left, right[...], preferred_element_type=jnp.float32)


def first_products(order, latents, out_grads):
    tok, wide = out_grads.shape
    ins = [(out_grads, resident(out_grads))]
    for job in SETS_A:
        at = lambda i, t, w, job=job: (0, t[spot(w, job[0], job[2], job[1], i)] >> 2)
        ins.append((latents, spec((tok, BLK), at)))
    outs = [((wide, tok), spec((wide, tok), lambda i, t, w: (0, 0)), out_grads.dtype)]
    for _ in SETS_A:
        outs.append(((4, ROWS_A, BLK), spec((1, ROWS_A, BLK), lambda i, t, w: (i, 0, 0))))
    return order(first_body, 4, ins, outs, vmem=LARGE)


def products_body(jobs, table, where, turned, latents, *refs):
    outs, got = refs[-len(jobs) :], refs[: -len(jobs)]
    i = pl.program_id(0)
    for m, ((stream, sub, r), out) in enumerate(zip(jobs, outs)):
        n, rows = out.shape[:2]
        for u in range(n):
            at = spot(where, stream, r, sub, n * i + u)
            value = piece(turned, latents, table[at], ROW[stream], rows)
            if m < len(got):
                value = value + got[m][u]
            out[u] = value


def products(order, turned, latents, jobs, got=()):
    outs = []
    for stream, sub, r in jobs:
        n, rows = (4, ROWS_A) if stream in "xy" else (16, 2 * ROWS_C)
        outs.append(((n, rows, BLK), spec((n // 4, rows, BLK), lambda i, t, w: (i, 0, 0))))
    return order(
        functools.partial(products_body, jobs),
        4,
        [(turned, resident(turned)), (latents, resident(latents))]
        + [(g, spec((1, ROWS_A, BLK), lambda i, t, w: (i, 0, 0))) for g in got],
        outs,
        vmem=LARGE,
    )


def whole(array):
    zeros = (0,) * array.ndim
    return spec(array.shape, lambda i, t, w: zeros)


def full(*shape):
    zeros = (0,) * len(shape)
    return (shape, spec(shape, lambda i, t, w: zeros))


def relay_body(table, where, *refs):
    for got, term, out in zip(refs[:4], refs[4:8], refs[8:]):
        out[...] = got[...] + term[...]


def relay(order, got, terms):
    here = spec((1, ROWS_A, BLK), lambda i, t, w: (i, 0, 0))
    ins = [(a, here) for a in (*got, *terms)]
    return order(relay_body, 4, ins, [(got[0].shape, here)] * 4, vmem=LARGE)


def half_rows(stream):
    return ROWS_A + 2 * (ROWS_C + (EXTRA if stream == "x" else 0))


MESSAGES = ((2, 0, (0, 0)), (1, 1, (0, 1)), (2, 1, (1, 0)), (3, 0, (1, 1)))
TERMS = ((1, 0, (0,)), (3, 1, (1,)), (0, 0, (2, 0)), (0, 1, (2, 1)))


def turn_body(jobs, table, where, *refs):
    sums, refs = refs[:3], refs[3:]
    ins, outs = refs[: 4 * len(jobs)], refs[4 * len(jobs) :]
    for n, (stream, r, half, place) in enumerate(jobs):
        base, more, got, term = ins[4 * n : 4 * n + 4]
        out = outs[place[0]].at[place[1]] if len(place) == 2 else outs[place[0]]
        out[:ROWS_A, :] = base[0] + more[0]
        rows = (half_rows(stream) - ROWS_A) // 2
        for v in range(2):
            at = (0, v) if stream == "y" else (v, 0)
            low = ROWS_A + v * rows
            out[low : low + ROWS_C, :] = got[at] + term[at]
            if stream == "y":
                continue
            first_in, second_in, sums_out = sums
            parts = []
            for sub in (1, 0):
                block = table[spot(where, "y", r, sub, 2 * half + v)]
                a = block >> 2
                parts.append(jnp.where(a < 4, first_in[a & 3], second_in[a & 3]))
                parts.append(sums_out[block & 3])
            parts.append(jnp.zeros((EXTRA - 4, BLK), jnp.float32))
            out[low + ROWS_C : low + rows, :] = jnp.concatenate(parts, axis=0)


def turn(order, streams, pieces, halves, got, terms, sums):
    once = dict(pipeline_mode=pl.Buffered(1))
    ins = [(s, whole(s)) for s in sums]
    jobs, outs = [], []
    for stream in streams:
        for r, half, place in pieces:
            jobs.append((stream, r, half, (place[0] + len(outs), *place[1:])))
            if stream == "x":
                here = lambda i, t, w, r=r: ((w[2] + r) & 3, 0, 0)
                shape = (2, 1, ROWS_C, BLK)
                side = lambda i, t, w, r=r, h=half: (h, (w[2] + r) & 3, 1, 0)
            else:
                here = lambda i, t, w, r=r: ((w[0] + r) & 3, 0, 0)
                shape = (1, 2, ROWS_C, BLK)
                side = lambda i, t, w, r=r, h=half: ((w[0] + r) & 3, h, 0, 0)
            ins += [(a, spec((1, ROWS_A, BLK), here, **once)) for a in halves[stream][half]]
            for a in (got, terms):
                ins.append((a.reshape(4, 4, 2 * ROWS_C, BLK), spec(shape, side, **once)))
        rows = half_rows(stream)
        if pieces is TERMS:
            outs += [full(rows, BLK)] * 2 + [full(2, rows, BLK)]
        else:
            outs += [full(2, rows, BLK)] * 2
    return order(functools.partial(turn_body, jobs), 1, ins, outs, vmem=TURN)


def relay_half_body(table, where, message, term, out):
    out[...] = message[0] + term[...]


def relay_half(order, message, term):
    rows = message.shape[1]
    ins = [(message, spec((1, rows, BLK), lambda i, t, w: (0, 0, 0))), (term, whole(term))]
    return order(relay_half_body, 1, ins, [full(rows, BLK)])[0]


def end_body(stream, table, where, own, forth, back, more_forth, more_back, *outs):
    halves = (
        lambda a, b: own[0, a:b] + back[1, a:b] + more_forth[a:b, :],
        lambda a, b: own[1, a:b] + forth[1, a:b] + more_back[a:b, :],
    )
    outs[0][...] = halves[0](0, ROWS_A)
    outs[1][...] = halves[1](0, ROWS_A)
    rows = (half_rows(stream) - ROWS_A) // 2
    for u in range(4):
        base = ROWS_A + (u % 2) * rows
        slot = halves[u // 2](base, base + rows)
        for d in range(4):

            @pl.when(((where[0 if stream == "x" else 2] + d) & 3) == u)
            def _():
                outs[2 + d][...] = slot


def end(order, stream, own, forth, back, more_forth, more_back):
    rows = (half_rows(stream) - ROWS_A) // 2
    outs = [full(ROWS_A, BLK)] * 2 + [full(rows, BLK)] * 4
    ins = [(a, whole(a)) for a in (own, forth, back, more_forth, more_back)]
    return order(functools.partial(end_body, stream), 1, ins, outs)


def sums_body(table, where, rows, basis, out):
    high, low = split(basis[0])
    tokens = rows[...]
    moved = jnp.dot(
        jnp.concatenate([tokens, tokens], axis=1),
        jnp.concatenate([high, low], axis=0),
        preferred_element_type=jnp.float32,
    )
    out[0] = jnp.sum(moved * moved, axis=0, keepdims=True)


def square_sums(order, rows, basis, first, n):
    tok = rows.shape[0]
    ins = [
        (rows, spec((tok, BLK), lambda i, t, w: (0, first + i))),
        (basis, spec((1, BLK, BLK), lambda i, t, w: (first + i, 0, 0))),
    ]
    out = ((n, 1, BLK), spec((1, 1, BLK), lambda i, t, w: (i, 0, 0)))
    return order(sums_body, n, ins, [out], vmem=SMALL)[0]


def total_body(table, where, *refs):
    value = (refs[0][...] + refs[1][...]) + (refs[2][...] + refs[3][...])
    refs[4][...] = value[:ROWS_C]
    if len(refs) == 6:
        refs[5][...] = value[ROWS_C:]


def total(order, parts):
    rows = parts[0].shape[0]
    outs = [full(ROWS_C, BLK)] + ([full(EXTRA, BLK)] if rows > ROWS_C else [])
    return order(total_body, 1, [(p, whole(p)) for p in parts], outs)


def mine(w):
    return w[0] * 8 + (1 - w[1]) * 4 + w[2]


def rotate_body(joined, table, where, first, second, basis, out):
    a = split(basis[0])
    if joined:
        value = first[...] + second[...]
    else:
        value = jnp.concatenate([first[...], second[...]], axis=0)
    out[...] = dot3(split(value), a, ((1,), (0,)))


def rotate(order, first, second, eig_in, joined):
    ins = [(a, whole(a)) for a in (first, second)]
    ins.append((eig_in, spec((1, BLK, BLK), lambda i, t, w: (t[mine(w)] >> 2, 0, 0))))
    rows = first.shape[0] * (1 if joined else 2)
    body = functools.partial(rotate_body, joined)
    return order(body, 1, ins, [full(rows, BLK)], vmem=TURN)[0]


def precondition_body(tokens_all, table, where, *refs):
    x, c, y0, y1, ours, theirs = (r[...] for r in refs[:6])
    basis_in, basis_out, out = refs[6:]
    scale = 1.0 / tokens_all
    values_in = (ours[0:1] + theirs[2:3]) * scale
    values_out = (ours[1:2] + theirs[3:4]) * scale
    a = split(basis_in[0])
    b = split(basis_out[0])
    y = dot3(split(y0 + y1), a, ((1,), (0,)))
    rotated = jnp.concatenate([x, y, c], axis=0) * scale
    rotated = dot3(b, split(rotated), ((0,), (0,)))
    scaled = rotated / (values_out.reshape(BLK, 1) * values_in + DAMPING)
    back = dot3(b, split(scaled), ((1,), (0,)))
    out[...] = dot3(a, split(back), ((1,), (1,)))


def precondition(tokens_all, order, parts, eig_in, eig_out):
    ins = [(q, whole(q)) for q in parts]
    ins.append((eig_in, spec((1, BLK, BLK), lambda i, t, w: (t[mine(w)] >> 2, 0, 0))))
    ins.append((eig_out, spec((1, BLK, BLK), lambda i, t, w: (t[mine(w)] & 3, 0, 0))))
    return order(
        functools.partial(precondition_body, tokens_all),
        1,
        ins,
        [full(BLK, BLK)],
        vmem=TURN,
    )[0]


def on_device(latents, out_grads, eig_in, eig_out, table):
    tokens_all = latents.shape[0] * N_TM
    tm = lax.axis_index("tm")
    fsdp = lax.axis_index("fsdp")
    x, zl, y = tm // 8, (tm // 4) % 2, tm % 4
    zh, core = fsdp // 2, fsdp % 2
    where = jnp.stack([x, zl, y]).astype(jnp.int32)
    near, cross = pairs_z(1), pairs_z(-1)
    send = lambda value, pairs: lax.ppermute(value, AXES, pairs)
    hop = lambda value, axis, d: send(value, pairs_far(axis, d))
    both = lambda forth, back, axis: [hop(forth, axis, 1), hop(back, axis, 3)]
    order = Order(table, where)
    far = lambda parts, axis: [parts[0]] + [hop(parts[d], axis, d) for d in (1, 2, 3)]

    turned, *sets_a = first_products(order, latents, out_grads)
    got_a = both(*sets_a[:2], "x") + both(*sets_a[2:], "y")
    got_c = send(products(order, turned, latents, SETS_AWAY)[0], near)
    made = products(order, turned, latents, SETS_B + SETS_T)
    got_b = both(*made[:2], "x") + both(*made[2:4], "y")
    sets_t = relay(order, got_a, made[4:])
    sums = [square_sums(order, latents, eig_in, 0, 4)]
    got_t = both(*order.gate(sets_t[:2], got_b[:2]), "x")
    got_t += both(*order.gate(sets_t[2:], got_b[2:]), "y")
    got_b = [got_b[n] for n in (1, 0, 3, 2)]
    *own, terms_c = products(order, turned, latents, SETS_OWN + SETS_KEEP, got_b)
    sums.append(square_sums(order, latents, eig_in, 4, 4))
    sums.append(square_sums(order, out_grads, eig_out, 0, 4))

    halves = {
        stream: ((own[n], got_t[n]), (own[n + 1], got_t[n + 1]))
        for n, stream in ((0, "x"), (2, "y"))
    }
    rest = (halves, got_c, terms_c, sums)
    messages = turn(order, "xy", MESSAGES, *rest)
    msgs_x, msgs_y = both(*messages[:2], "y"), both(*messages[2:], "x")
    *parts_x, mine_x = turn(order, "x", TERMS, *rest)
    *parts_y, mine_y = turn(order, "y", TERMS, *rest)

    def follow(stream, messages, parts):
        more = [relay_half(order, m, p) for m, p in zip(messages, parts)]
        return both(*more, "y" if stream == "x" else "x")

    more_x = follow("x", msgs_x, parts_x)
    more_y = follow("y", msgs_y, parts_y)

    away_x, keep_x, *parts_cy = end(order, "x", mine_x, *msgs_x, *more_x)
    got_x = send(away_x, near)
    parts_cy = far(parts_cy, "x")
    order.also = [parts_cy[1], parts_cy[3]]
    away_y, keep_y, *parts_cx = end(order, "y", mine_y, *msgs_y, *more_y)
    got_y = send(away_y, near)
    done_cy, ours = total(order, parts_cy)
    theirs = send(ours, near)
    turned_x = rotate(order, keep_x, got_x, eig_in, True)
    (done_cx,) = total(order, far(parts_cx, "y"))
    turned_c = rotate(order, done_cx, done_cy, eig_in, False)
    update = precondition(
        tokens_all, order, [turned_x, turned_c, keep_y, got_y, ours, theirs], eig_in, eig_out
    )
    same = send(update, near)
    other = send(update, cross)
    same_core = send(same, pairs_core())
    other_core = send(other, pairs_core())
    result = jnp.zeros((N_FSDP, BLK, BLK), jnp.float32)
    for block, at in (
        (same, zh * 2 + core),
        (other, (1 - zh) * 2 + core),
        (same_core, zh * 2 + 1 - core),
        (other_core, (1 - zh) * 2 + 1 - core),
    ):
        result = lax.dynamic_update_index_in_dim(result, block, at, 0)
    return result[:, None]


def solution(mesh):
    in_specs = (P("tm", None), P("tm", "fsdp"), P(), P("fsdp", None, None), P())
    out_specs = P(None, "tm", None, None)
    return jax.shard_map(
        on_device, mesh=mesh, in_specs=in_specs, out_specs=out_specs, check_vma=False
    )
```

```python
import functools

import jax
import jax.numpy as jnp
from jax import lax
from jax.experimental import pallas as pl
from jax.experimental.pallas import tpu as pltpu
from jax.sharding import PartitionSpec as P

DAMPING = 0.0001
AXES = ("tm", "fsdp")
NX, NZ, NY = 4, 2, 4
N_TM, N_FSDP = 32, 4
BLK = 512
ROWS_A = 192
ROWS_C = (BLK - 2 * ROWS_A) // 2
EXTRA = 8
SMALL, TURN, LARGE = 16 * 1024 * 1024, 30 * 1024 * 1024, 56 * 1024 * 1024


def flat(x, zl, y, zh, core):
    return ((x % NX) * 8 + zl * 4 + (y % NY)) * N_FSDP + zh * 2 + core


def coords():
    for x in range(NX):
        for zl in range(NZ):
            for y in range(NY):
                for zh in range(2):
                    for core in range(2):
                        yield x, zl, y, zh, core


def pairs_far(axis, d):
    return [
        (flat(x, zl, y, zh, c), flat(x + d * (axis == "x"), zl, y + d * (axis == "y"), zh, c))
        for x, zl, y, zh, c in coords()
    ]


def pairs_z(step):
    out = []
    for x, zl, y, zh, c in coords():
        z = (zh * 2 + zl + (step if zl == 0 else -step)) % 4
        out.append((flat(x, zl, y, zh, c), flat(x, z % 2, y, z // 2, c)))
    return out


def pairs_core():
    return [
        (flat(x, zl, y, zh, c), flat(x, zl, y, zh, 1 - c))
        for x, zl, y, zh, c in coords()
    ]


def split(value):
    high = value.astype(jnp.bfloat16)
    low = (value - high.astype(jnp.float32)).astype(jnp.bfloat16)
    return high, low


def dot3(a, b, dims):
    (ah, al), (bh, bl) = a, b
    dot = functools.partial(
        lax.dot_general,
        dimension_numbers=(dims, ((), ())),
        preferred_element_type=jnp.float32,
    )
    return dot(ah, bh) + (dot(ah, bl) + dot(al, bh))


def spot(where, stream, r, sub, i):
    z = where[1] if sub == 0 else 1 - where[1]
    if stream == "x":
        return ((where[0] + r) & 3) * 8 + z * 4 + i
    if stream == "y":
        return i * 8 + z * 4 + ((where[2] + r) & 3)
    return (i >> 2) * 8 + z * 4 + (i & 3)


def spec(shape, index, **more):
    return pl.BlockSpec(shape, index, **more)


def resident(array):
    zeros = (0,) * array.ndim
    return pl.BlockSpec(array.shape, lambda *_: zeros, pipeline_mode=pl.Buffered(1))


class Order:
    def __init__(self, table, where):
        self.table, self.where, self.last = table, where, None
        self.also = []

    def gate(self, held, behind):
        anywhere = pl.BlockSpec(memory_space=pl.ANY)
        made = pl.pallas_call(
            lambda *refs: None,
            out_shape=[jax.ShapeDtypeStruct(a.shape, a.dtype) for a in held],
            in_specs=[anywhere] * (len(held) + len(behind) + 1),
            out_specs=[anywhere] * len(held),
            input_output_aliases={i: i for i in range(len(held))},
            cost_estimate=pl.CostEstimate(flops=0, bytes_accessed=1, transcendentals=0),
        )(*held, *behind, self.last)
        self.last = made[-1]
        return made

    def __call__(self, body, grid, ins, outs, cost=1.0, vmem=SMALL):
        shapes = [
            jax.ShapeDtypeStruct(o[0], o[2] if len(o) > 2 else jnp.float32) for o in outs
        ]
        inner = body
        if self.last is not None:
            after = [self.last] + self.also
            self.also = []
            ins = [(a, pl.BlockSpec(memory_space=pl.ANY)) for a in after] + ins
            inner = lambda table, where, *refs: body(table, where, *refs[len(after) :])
        made = pl.pallas_call(
            inner,
            out_shape=shapes,
            grid_spec=pltpu.PrefetchScalarGridSpec(
                num_scalar_prefetch=2,
                grid=(grid,),
                in_specs=[s for _, s in ins],
                out_specs=[o[1] for o in outs],
            ),
            cost_estimate=pl.CostEstimate(
                flops=0, bytes_accessed=int(cost * 3.69e6), transcendentals=0
            ),
            compiler_params=pltpu.CompilerParams(vmem_limit_bytes=vmem),
        )(self.table, self.where, *[a for a, _ in ins])
        self.last = made[-1]
        return made


def piece(turned, latents, block, row, rows):
    left = turned[pl.ds(pl.multiple_of((block & 3) * BLK + row, 16), rows), :]
    right = latents[:, pl.ds(pl.multiple_of((block >> 2) * BLK, BLK), BLK)]
    return jnp.dot(left, right, preferred_element_type=jnp.float32)


SETS_A = (("x", 0, 2), ("x", 1, 2), ("y", 0, 2), ("y", 1, 2))
SETS_B = (("x", 1, 1), ("x", 0, 3), ("y", 1, 1), ("y", 0, 3))
SETS_T = (("x", 0, 1), ("x", 1, 3), ("y", 0, 1), ("y", 1, 3))
SETS_OWN = (("x", 0, 0), ("x", 1, 0), ("y", 0, 0), ("y", 1, 0))
SETS_AWAY, SETS_KEEP = (("c", 0, 0),), (("c", 1, 0),)
ROW = {"x": 0, "y": ROWS_A, "c": 2 * ROWS_A}


def first_body(table, where, grads, *refs):
    rights, turned, outs = refs[:4], refs[4], refs[5:]
    i = pl.program_id(0)

    @pl.when(i == 0)
    def _():
        for c in range(grads.shape[1] // BLK):
            turned[c * BLK : (c + 1) * BLK, :] = grads[:, c * BLK : (c + 1) * BLK].T

    for right, out, (stream, sub, r) in zip(rights, outs, SETS_A):
        block = table[spot(where, stream, r, sub, i)]
        row = (block & 3) * BLK + ROW[stream]
        left = turned[pl.ds(pl.multiple_of(row, 16), ROWS_A), :]
        out[0] = jnp.dot(left, right[...], preferred_element_type=jnp.float32)


def first_products(order, latents, out_grads):
    tok, wide = out_grads.shape
    ins = [(out_grads, resident(out_grads))]
    for job in SETS_A:
        at = lambda i, t, w, job=job: (0, t[spot(w, job[0], job[2], job[1], i)] >> 2)
        ins.append((latents, spec((tok, BLK), at)))
    outs = [((wide, tok), spec((wide, tok), lambda i, t, w: (0, 0)), out_grads.dtype)]
    for _ in SETS_A:
        outs.append(((4, ROWS_A, BLK), spec((1, ROWS_A, BLK), lambda i, t, w: (i, 0, 0))))
    return order(first_body, 4, ins, outs, vmem=LARGE)


def products_body(jobs, table, where, turned, latents, *refs):
    outs, got = refs[-len(jobs) :], refs[: -len(jobs)]
    i = pl.program_id(0)
    for m, ((stream, sub, r), out) in enumerate(zip(jobs, outs)):
        n, rows = out.shape[:2]
        for u in range(n):
            at = spot(where, stream, r, sub, n * i + u)
            value = piece(turned, latents, table[at], ROW[stream], rows)
            if m < len(got):
                value = value + got[m][u]
            out[u] = value


def products(order, turned, latents, jobs, got=()):
    outs = []
    for stream, sub, r in jobs:
        n, rows = (4, ROWS_A) if stream in "xy" else (16, 2 * ROWS_C)
        outs.append(((n, rows, BLK), spec((n // 4, rows, BLK), lambda i, t, w: (i, 0, 0))))
    return order(
        functools.partial(products_body, jobs),
        4,
        [(turned, resident(turned)), (latents, resident(latents))]
        + [(g, spec((1, ROWS_A, BLK), lambda i, t, w: (i, 0, 0))) for g in got],
        outs,
        vmem=LARGE,
    )


def whole(array):
    zeros = (0,) * array.ndim
    return spec(array.shape, lambda i, t, w: zeros)


def full(*shape):
    zeros = (0,) * len(shape)
    return (shape, spec(shape, lambda i, t, w: zeros))


def relay_body(table, where, *refs):
    for got, term, out in zip(refs[:4], refs[4:8], refs[8:]):
        out[...] = got[...] + term[...]


def relay(order, got, terms):
    here = spec((1, ROWS_A, BLK), lambda i, t, w: (i, 0, 0))
    ins = [(a, here) for a in (*got, *terms)]
    return order(relay_body, 4, ins, [(got[0].shape, here)] * 4, vmem=LARGE)


def half_rows(stream):
    return ROWS_A + 2 * (ROWS_C + (EXTRA if stream == "x" else 0))


MESSAGES = ((2, 0, (0, 0)), (1, 1, (0, 1)), (2, 1, (1, 0)), (3, 0, (1, 1)))
TERMS = ((1, 0, (0,)), (3, 1, (1,)), (0, 0, (2, 0)), (0, 1, (2, 1)))


def turn_body(jobs, table, where, *refs):
    sums, refs = refs[:3], refs[3:]
    ins, outs = refs[: 4 * len(jobs)], refs[4 * len(jobs) :]
    for n, (stream, r, half, place) in enumerate(jobs):
        base, more, got, term = ins[4 * n : 4 * n + 4]
        out = outs[place[0]].at[place[1]] if len(place) == 2 else outs[place[0]]
        out[:ROWS_A, :] = base[0] + more[0]
        rows = (half_rows(stream) - ROWS_A) // 2
        for v in range(2):
            at = (0, v) if stream == "y" else (v, 0)
            low = ROWS_A + v * rows
            out[low : low + ROWS_C, :] = got[at] + term[at]
            if stream == "y":
                continue
            first_in, second_in, sums_out = sums
            parts = []
            for sub in (1, 0):
                block = table[spot(where, "y", r, sub, 2 * half + v)]
                a = block >> 2
                parts.append(jnp.where(a < 4, first_in[a & 3], second_in[a & 3]))
                parts.append(sums_out[block & 3])
            parts.append(jnp.zeros((EXTRA - 4, BLK), jnp.float32))
            out[low + ROWS_C : low + rows, :] = jnp.concatenate(parts, axis=0)


def turn(order, streams, pieces, halves, got, terms, sums):
    once = dict(pipeline_mode=pl.Buffered(1))
    ins = [(s, whole(s)) for s in sums]
    jobs, outs = [], []
    for stream in streams:
        for r, half, place in pieces:
            jobs.append((stream, r, half, (place[0] + len(outs), *place[1:])))
            if stream == "x":
                here = lambda i, t, w, r=r: ((w[2] + r) & 3, 0, 0)
                shape = (2, 1, ROWS_C, BLK)
                side = lambda i, t, w, r=r, h=half: (h, (w[2] + r) & 3, 1, 0)
            else:
                here = lambda i, t, w, r=r: ((w[0] + r) & 3, 0, 0)
                shape = (1, 2, ROWS_C, BLK)
                side = lambda i, t, w, r=r, h=half: ((w[0] + r) & 3, h, 0, 0)
            ins += [(a, spec((1, ROWS_A, BLK), here, **once)) for a in halves[stream][half]]
            for a in (got, terms):
                ins.append((a.reshape(4, 4, 2 * ROWS_C, BLK), spec(shape, side, **once)))
        rows = half_rows(stream)
        if pieces is TERMS:
            outs += [full(rows, BLK)] * 2 + [full(2, rows, BLK)]
        else:
            outs += [full(2, rows, BLK)] * 2
    return order(functools.partial(turn_body, jobs), 1, ins, outs, vmem=TURN)


def relay_half_body(table, where, message, term, out):
    out[...] = message[0] + term[...]


def relay_half(order, message, term):
    rows = message.shape[1]
    ins = [(message, spec((1, rows, BLK), lambda i, t, w: (0, 0, 0))), (term, whole(term))]
    return order(relay_half_body, 1, ins, [full(rows, BLK)])[0]


def end_body(stream, table, where, own, forth, back, more_forth, more_back, *outs):
    halves = (
        lambda a, b: own[0, a:b] + back[1, a:b] + more_forth[a:b, :],
        lambda a, b: own[1, a:b] + forth[1, a:b] + more_back[a:b, :],
    )
    outs[0][...] = halves[0](0, ROWS_A)
    outs[1][...] = halves[1](0, ROWS_A)
    rows = (half_rows(stream) - ROWS_A) // 2
    for u in range(4):
        base = ROWS_A + (u % 2) * rows
        slot = halves[u // 2](base, base + rows)
        for d in range(4):

            @pl.when(((where[0 if stream == "x" else 2] + d) & 3) == u)
            def _():
                outs[2 + d][...] = slot


def end(order, stream, own, forth, back, more_forth, more_back):
    rows = (half_rows(stream) - ROWS_A) // 2
    outs = [full(ROWS_A, BLK)] * 2 + [full(rows, BLK)] * 4
    ins = [(a, whole(a)) for a in (own, forth, back, more_forth, more_back)]
    return order(functools.partial(end_body, stream), 1, ins, outs)


def sums_body(table, where, rows, basis, out):
    high, low = split(basis[0])
    tokens = rows[...]
    moved = jnp.dot(
        jnp.concatenate([tokens, tokens], axis=1),
        jnp.concatenate([high, low], axis=0),
        preferred_element_type=jnp.float32,
    )
    out[0] = jnp.sum(moved * moved, axis=0, keepdims=True)


def square_sums(order, rows, basis, first, n):
    tok = rows.shape[0]
    ins = [
        (rows, spec((tok, BLK), lambda i, t, w: (0, first + i))),
        (basis, spec((1, BLK, BLK), lambda i, t, w: (first + i, 0, 0))),
    ]
    out = ((n, 1, BLK), spec((1, 1, BLK), lambda i, t, w: (i, 0, 0)))
    return order(sums_body, n, ins, [out], vmem=SMALL)[0]


def total_body(table, where, *refs):
    value = (refs[0][...] + refs[1][...]) + (refs[2][...] + refs[3][...])
    refs[4][...] = value[:ROWS_C]
    if len(refs) == 6:
        refs[5][...] = value[ROWS_C:]


def total(order, parts):
    rows = parts[0].shape[0]
    outs = [full(ROWS_C, BLK)] + ([full(EXTRA, BLK)] if rows > ROWS_C else [])
    return order(total_body, 1, [(p, whole(p)) for p in parts], outs)


def mine(w):
    return w[0] * 8 + (1 - w[1]) * 4 + w[2]


def bases_body(table, where, basis_in, basis_out, *outs):
    outs[0][...], outs[1][...] = split(basis_in[0])
    outs[2][...], outs[3][...] = split(basis_out[0])


def bases(order, eig_in, eig_out):
    ins = [
        (eig_in, spec((1, BLK, BLK), lambda i, t, w: (t[mine(w)] >> 2, 0, 0))),
        (eig_out, spec((1, BLK, BLK), lambda i, t, w: (t[mine(w)] & 3, 0, 0))),
    ]
    outs = [(*full(BLK, BLK), jnp.bfloat16)] * 4
    made = order(bases_body, 1, ins, outs)
    return made[:2], made[2:]


def rotate_body(table, where, high, low, *refs):
    parts, out = refs[:-1], refs[-1]
    value = parts[0][...] + parts[1][...]
    if len(parts) > 2:
        value = value + (parts[2][...] + parts[3][...])
        value = jnp.concatenate([value, parts[4][...]], axis=0)
    out[...] = dot3(split(value), (high[...], low[...]), ((1,), (0,)))


def rotate(order, basis, parts):
    ins = [(a, whole(a)) for a in (*basis, *parts)]
    rows = parts[0].shape[0] * (1 if len(parts) == 2 else 2)
    return order(rotate_body, 1, ins, [full(rows, BLK)])[0]


def precondition_body(tokens_all, table, where, *refs):
    x, c, y0, y1, ours, theirs = (r[...] for r in refs[:6])
    a, b = (refs[6][...], refs[7][...]), (refs[8][...], refs[9][...])
    out = refs[10]
    scale = 1.0 / tokens_all
    values_in = (ours[0:1] + theirs[2:3]) * scale
    values_out = (ours[1:2] + theirs[3:4]) * scale
    y = dot3(split(y0 + y1), a, ((1,), (0,)))
    rotated = jnp.concatenate([x, y, c], axis=0) * scale
    rotated = dot3(b, split(rotated), ((0,), (0,)))
    scaled = rotated / (values_out.reshape(BLK, 1) * values_in + DAMPING)
    back = dot3(b, split(scaled), ((1,), (0,)))
    out[...] = dot3(a, split(back), ((1,), (1,)))


def precondition(tokens_all, order, parts, basis_in, basis_out):
    ins = [(q, whole(q)) for q in (*parts, *basis_in, *basis_out)]
    return order(
        functools.partial(precondition_body, tokens_all),
        1,
        ins,
        [full(BLK, BLK)],
        vmem=TURN,
    )[0]


def on_device(latents, out_grads, eig_in, eig_out, table):
    tokens_all = latents.shape[0] * N_TM
    tm = lax.axis_index("tm")
    fsdp = lax.axis_index("fsdp")
    x, zl, y = tm // 8, (tm // 4) % 2, tm % 4
    zh, core = fsdp // 2, fsdp % 2
    where = jnp.stack([x, zl, y]).astype(jnp.int32)
    near, cross = pairs_z(1), pairs_z(-1)
    send = lambda value, pairs: lax.ppermute(value, AXES, pairs)
    hop = lambda value, axis, d: send(value, pairs_far(axis, d))
    both = lambda forth, back, axis: [hop(forth, axis, 1), hop(back, axis, 3)]
    order = Order(table, where)
    far = lambda parts, axis: [parts[0]] + [hop(parts[d], axis, d) for d in (1, 2, 3)]

    turned, *sets_a = first_products(order, latents, out_grads)
    got_a = both(*sets_a[:2], "x") + both(*sets_a[2:], "y")
    got_c = send(products(order, turned, latents, SETS_AWAY)[0], near)
    made = products(order, turned, latents, SETS_B + SETS_T)
    got_b = both(*made[:2], "x") + both(*made[2:4], "y")
    sets_t = relay(order, got_a, made[4:])
    sums = [square_sums(order, latents, eig_in, 0, 4)]
    basis_in, basis_out = bases(order, eig_in, eig_out)
    got_t = both(*order.gate(sets_t[:2], got_b[:2]), "x")
    got_t += both(*order.gate(sets_t[2:], got_b[2:]), "y")
    got_b = [got_b[n] for n in (1, 0, 3, 2)]
    *own, terms_c = products(order, turned, latents, SETS_OWN + SETS_KEEP, got_b)
    sums.append(square_sums(order, latents, eig_in, 4, 4))
    sums.append(square_sums(order, out_grads, eig_out, 0, 4))

    halves = {
        stream: ((own[n], got_t[n]), (own[n + 1], got_t[n + 1]))
        for n, stream in ((0, "x"), (2, "y"))
    }
    rest = (halves, got_c, terms_c, sums)
    messages = turn(order, "xy", MESSAGES, *rest)
    msgs_x, msgs_y = both(*messages[:2], "y"), both(*messages[2:], "x")
    *parts_x, mine_x = turn(order, "x", TERMS, *rest)
    *parts_y, mine_y = turn(order, "y", TERMS, *rest)

    def follow(stream, messages, parts):
        more = [relay_half(order, m, p) for m, p in zip(messages, parts)]
        return both(*more, "y" if stream == "x" else "x")

    more_x = follow("x", msgs_x, parts_x)
    more_y = follow("y", msgs_y, parts_y)

    away_x, keep_x, *parts_cy = end(order, "x", mine_x, *msgs_x, *more_x)
    got_x = send(away_x, near)
    parts_cy = far(parts_cy, "x")
    order.also = [parts_cy[1], parts_cy[3]]
    away_y, keep_y, *parts_cx = end(order, "y", mine_y, *msgs_y, *more_y)
    got_y = send(away_y, near)
    turned_x = rotate(order, basis_in, [keep_x, got_x])
    done_cy, ours = total(order, parts_cy)
    theirs = send(ours, near)
    turned_c = rotate(order, basis_in, [*far(parts_cx, "y"), done_cy])
    update = precondition(
        tokens_all,
        order,
        [turned_x, turned_c, keep_y, got_y, ours, theirs],
        basis_in,
        basis_out,
    )
    same = send(update, near)
    other = send(update, cross)
    same_core = send(same, pairs_core())
    other_core = send(other, pairs_core())
    result = jnp.zeros((N_FSDP, BLK, BLK), jnp.float32)
    for block, at in (
        (same, zh * 2 + core),
        (other, (1 - zh) * 2 + core),
        (same_core, zh * 2 + 1 - core),
        (other_core, (1 - zh) * 2 + 1 - core),
    ):
        result = lax.dynamic_update_index_in_dim(result, block, at, 0)
    return result[:, None]


def solution(mesh):
    in_specs = (P("tm", None), P("tm", "fsdp"), P(), P("fsdp", None, None), P())
    out_specs = P(None, "tm", None, None)
    return jax.shard_map(
        on_device, mesh=mesh, in_specs=in_specs, out_specs=out_specs, check_vma=False
    )
```

```python
import functools

import jax
import jax.numpy as jnp
from jax import lax
from jax.experimental import pallas as pl
from jax.experimental.pallas import tpu as pltpu
from jax.sharding import PartitionSpec as P

DAMPING = 0.0001
AXES = ("tm", "fsdp")
NX, NZ, NY = 4, 2, 4
N_TM, N_FSDP = 32, 4
BLK = 512
ROWS_A = 192
ROWS_C = (BLK - 2 * ROWS_A) // 2
EXTRA = 8
SMALL, TURN, LARGE = 16 * 1024 * 1024, 30 * 1024 * 1024, 56 * 1024 * 1024


def flat(x, zl, y, zh, core):
    return ((x % NX) * 8 + zl * 4 + (y % NY)) * N_FSDP + zh * 2 + core


def coords():
    for x in range(NX):
        for zl in range(NZ):
            for y in range(NY):
                for zh in range(2):
                    for core in range(2):
                        yield x, zl, y, zh, core


def pairs_far(axis, d):
    return [
        (flat(x, zl, y, zh, c), flat(x + d * (axis == "x"), zl, y + d * (axis == "y"), zh, c))
        for x, zl, y, zh, c in coords()
    ]


def pairs_z(step):
    out = []
    for x, zl, y, zh, c in coords():
        z = (zh * 2 + zl + (step if zl == 0 else -step)) % 4
        out.append((flat(x, zl, y, zh, c), flat(x, z % 2, y, z // 2, c)))
    return out


def pairs_core():
    return [
        (flat(x, zl, y, zh, c), flat(x, zl, y, zh, 1 - c))
        for x, zl, y, zh, c in coords()
    ]


def split(value):
    high = value.astype(jnp.bfloat16)
    low = (value - high.astype(jnp.float32)).astype(jnp.bfloat16)
    return high, low


def dot3(a, b, dims):
    (ah, al), (bh, bl) = a, b
    dot = functools.partial(
        lax.dot_general,
        dimension_numbers=(dims, ((), ())),
        preferred_element_type=jnp.float32,
    )
    return dot(ah, bh) + (dot(ah, bl) + dot(al, bh))


def spot(where, stream, r, sub, i):
    z = where[1] if sub == 0 else 1 - where[1]
    if stream == "x":
        return ((where[0] + r) & 3) * 8 + z * 4 + i
    if stream == "y":
        return i * 8 + z * 4 + ((where[2] + r) & 3)
    return (i >> 2) * 8 + z * 4 + (i & 3)


def spec(shape, index, **more):
    return pl.BlockSpec(shape, index, **more)


def resident(array):
    zeros = (0,) * array.ndim
    return pl.BlockSpec(array.shape, lambda *_: zeros, pipeline_mode=pl.Buffered(1))


class Order:
    def __init__(self, table, where):
        self.table, self.where, self.last = table, where, None
        self.also = []

    def gate(self, held, behind):
        anywhere = pl.BlockSpec(memory_space=pl.ANY)
        made = pl.pallas_call(
            lambda *refs: None,
            out_shape=[jax.ShapeDtypeStruct(a.shape, a.dtype) for a in held],
            in_specs=[anywhere] * (len(held) + len(behind) + 1),
            out_specs=[anywhere] * len(held),
            input_output_aliases={i: i for i in range(len(held))},
            cost_estimate=pl.CostEstimate(flops=0, bytes_accessed=1, transcendentals=0),
        )(*held, *behind, self.last)
        self.last = made[-1]
        return made

    def __call__(self, body, grid, ins, outs, cost=1.0, vmem=SMALL):
        shapes = [
            jax.ShapeDtypeStruct(o[0], o[2] if len(o) > 2 else jnp.float32) for o in outs
        ]
        inner = body
        if self.last is not None:
            after = [self.last] + self.also
            self.also = []
            ins = [(a, pl.BlockSpec(memory_space=pl.ANY)) for a in after] + ins
            inner = lambda table, where, *refs: body(table, where, *refs[len(after) :])
        made = pl.pallas_call(
            inner,
            out_shape=shapes,
            grid_spec=pltpu.PrefetchScalarGridSpec(
                num_scalar_prefetch=2,
                grid=(grid,),
                in_specs=[s for _, s in ins],
                out_specs=[o[1] for o in outs],
            ),
            cost_estimate=pl.CostEstimate(
                flops=0, bytes_accessed=int(cost * 3.69e6), transcendentals=0
            ),
            compiler_params=pltpu.CompilerParams(vmem_limit_bytes=vmem),
        )(self.table, self.where, *[a for a, _ in ins])
        self.last = made[-1]
        return made


def piece(turned, latents, block, row, rows):
    left = turned[pl.ds(pl.multiple_of((block & 3) * BLK + row, 16), rows), :]
    right = latents[:, pl.ds(pl.multiple_of((block >> 2) * BLK, BLK), BLK)]
    return jnp.dot(left, right, preferred_element_type=jnp.float32)


SETS_A = (("x", 0, 2), ("x", 1, 2), ("y", 0, 2), ("y", 1, 2))
SETS_B = (("x", 1, 1), ("x", 0, 3), ("y", 1, 1), ("y", 0, 3))
SETS_T = (("x", 0, 1), ("x", 1, 3), ("y", 0, 1), ("y", 1, 3))
SETS_OWN = (("x", 0, 0), ("x", 1, 0), ("y", 0, 0), ("y", 1, 0))
SETS_AWAY, SETS_KEEP = (("c", 0, 0),), (("c", 1, 0),)
ROW = {"x": 0, "y": ROWS_A, "c": 2 * ROWS_A}


def first_body(table, where, grads, *refs):
    rights, turned, outs = refs[:4], refs[4], refs[5:]
    i = pl.program_id(0)

    @pl.when(i == 0)
    def _():
        for c in range(grads.shape[1] // BLK):
            turned[c * BLK : (c + 1) * BLK, :] = grads[:, c * BLK : (c + 1) * BLK].T

    for right, out, (stream, sub, r) in zip(rights, outs, SETS_A):
        block = table[spot(where, stream, r, sub, i)]
        row = (block & 3) * BLK + ROW[stream]
        left = turned[pl.ds(pl.multiple_of(row, 16), ROWS_A), :]
        out[0] = jnp.dot(left, right[...], preferred_element_type=jnp.float32)


def first_products(order, latents, out_grads):
    tok, wide = out_grads.shape
    ins = [(out_grads, resident(out_grads))]
    for job in SETS_A:
        at = lambda i, t, w, job=job: (0, t[spot(w, job[0], job[2], job[1], i)] >> 2)
        ins.append((latents, spec((tok, BLK), at)))
    outs = [((wide, tok), spec((wide, tok), lambda i, t, w: (0, 0)), out_grads.dtype)]
    for _ in SETS_A:
        outs.append(((4, ROWS_A, BLK), spec((1, ROWS_A, BLK), lambda i, t, w: (i, 0, 0))))
    return order(first_body, 4, ins, outs, vmem=LARGE)


def products_body(jobs, table, where, turned, latents, *refs):
    outs, got = refs[-len(jobs) :], refs[: -len(jobs)]
    i = pl.program_id(0)
    for m, ((stream, sub, r), out) in enumerate(zip(jobs, outs)):
        n, rows = out.shape[:2]
        for u in range(n):
            at = spot(where, stream, r, sub, n * i + u)
            value = piece(turned, latents, table[at], ROW[stream], rows)
            if m < len(got):
                value = value + got[m][u]
            out[u] = value


def products(order, turned, latents, jobs, got=()):
    outs = []
    for stream, sub, r in jobs:
        n, rows = (4, ROWS_A) if stream in "xy" else (16, 2 * ROWS_C)
        outs.append(((n, rows, BLK), spec((n // 4, rows, BLK), lambda i, t, w: (i, 0, 0))))
    return order(
        functools.partial(products_body, jobs),
        4,
        [(turned, resident(turned)), (latents, resident(latents))]
        + [(g, spec((1, ROWS_A, BLK), lambda i, t, w: (i, 0, 0))) for g in got],
        outs,
        vmem=LARGE,
    )


def whole(array):
    zeros = (0,) * array.ndim
    return spec(array.shape, lambda i, t, w: zeros)


def full(*shape):
    zeros = (0,) * len(shape)
    return (shape, spec(shape, lambda i, t, w: zeros))


def relay_body(table, where, *refs):
    for got, term, out in zip(refs[:4], refs[4:8], refs[8:]):
        out[...] = got[...] + term[...]


def relay(order, got, terms):
    here = spec((1, ROWS_A, BLK), lambda i, t, w: (i, 0, 0))
    ins = [(a, here) for a in (*got, *terms)]
    return order(relay_body, 4, ins, [(got[0].shape, here)] * 4, vmem=LARGE)


def half_rows(stream):
    return ROWS_A + 2 * (ROWS_C + (EXTRA if stream == "x" else 0))


MESSAGES = ((2, 0, (0, 0)), (1, 1, (0, 1)), (2, 1, (1, 0)), (3, 0, (1, 1)))
TERMS = ((1, 0, (0,)), (3, 1, (1,)), (0, 0, (2, 0)), (0, 1, (2, 1)))


def turn_body(jobs, table, where, *refs):
    sums, refs = refs[:3], refs[3:]
    ins, outs = refs[: 4 * len(jobs)], refs[4 * len(jobs) :]
    for n, (stream, r, half, place) in enumerate(jobs):
        base, more, got, term = ins[4 * n : 4 * n + 4]
        out = outs[place[0]].at[place[1]] if len(place) == 2 else outs[place[0]]
        out[:ROWS_A, :] = base[0] + more[0]
        rows = (half_rows(stream) - ROWS_A) // 2
        for v in range(2):
            at = (0, v) if stream == "y" else (v, 0)
            low = ROWS_A + v * rows
            out[low : low + ROWS_C, :] = got[at] + term[at]
            if stream == "y":
                continue
            first_in, second_in, sums_out = sums
            parts = []
            for sub in (1, 0):
                block = table[spot(where, "y", r, sub, 2 * half + v)]
                a = block >> 2
                parts.append(jnp.where(a < 4, first_in[a & 3], second_in[a & 3]))
                parts.append(sums_out[block & 3])
            parts.append(jnp.zeros((EXTRA - 4, BLK), jnp.float32))
            out[low + ROWS_C : low + rows, :] = jnp.concatenate(parts, axis=0)


def turn(order, streams, pieces, halves, got, terms, sums):
    once = dict(pipeline_mode=pl.Buffered(1))
    ins = [(s, whole(s)) for s in sums]
    jobs, outs = [], []
    for stream in streams:
        for r, half, place in pieces:
            jobs.append((stream, r, half, (place[0] + len(outs), *place[1:])))
            if stream == "x":
                here = lambda i, t, w, r=r: ((w[2] + r) & 3, 0, 0)
                shape = (2, 1, ROWS_C, BLK)
                side = lambda i, t, w, r=r, h=half: (h, (w[2] + r) & 3, 1, 0)
            else:
                here = lambda i, t, w, r=r: ((w[0] + r) & 3, 0, 0)
                shape = (1, 2, ROWS_C, BLK)
                side = lambda i, t, w, r=r, h=half: ((w[0] + r) & 3, h, 0, 0)
            ins += [(a, spec((1, ROWS_A, BLK), here, **once)) for a in halves[stream][half]]
            for a in (got, terms):
                ins.append((a.reshape(4, 4, 2 * ROWS_C, BLK), spec(shape, side, **once)))
        rows = half_rows(stream)
        if pieces is TERMS:
            outs += [full(rows, BLK)] * 2 + [full(2, rows, BLK)]
        else:
            outs += [full(2, rows, BLK)] * 2
    return order(functools.partial(turn_body, jobs), 1, ins, outs, vmem=TURN)


def relay_half_body(table, where, message, term, out):
    out[...] = message[0] + term[...]


def relay_half(order, message, term):
    rows = message.shape[1]
    ins = [(message, spec((1, rows, BLK), lambda i, t, w: (0, 0, 0))), (term, whole(term))]
    return order(relay_half_body, 1, ins, [full(rows, BLK)])[0]


def end_body(stream, table, where, own, forth, back, more_forth, more_back, *outs):
    halves = (
        lambda a, b: own[0, a:b] + back[1, a:b] + more_forth[a:b, :],
        lambda a, b: own[1, a:b] + forth[1, a:b] + more_back[a:b, :],
    )
    outs[0][...] = halves[0](0, ROWS_A)
    outs[1][...] = halves[1](0, ROWS_A)
    rows = (half_rows(stream) - ROWS_A) // 2
    for u in range(4):
        base = ROWS_A + (u % 2) * rows
        slot = halves[u // 2](base, base + rows)
        for d in range(4):

            @pl.when(((where[0 if stream == "x" else 2] + d) & 3) == u)
            def _():
                outs[2 + d][...] = slot


def end(order, stream, own, forth, back, more_forth, more_back):
    rows = (half_rows(stream) - ROWS_A) // 2
    outs = [full(ROWS_A, BLK)] * 2 + [full(rows, BLK)] * 4
    ins = [(a, whole(a)) for a in (own, forth, back, more_forth, more_back)]
    return order(functools.partial(end_body, stream), 1, ins, outs)


def sums_body(table, where, rows, basis, out):
    high, low = split(basis[0])
    tokens = rows[...]
    moved = jnp.dot(
        jnp.concatenate([tokens, tokens], axis=1),
        jnp.concatenate([high, low], axis=0),
        preferred_element_type=jnp.float32,
    )
    out[0] = jnp.sum(moved * moved, axis=0, keepdims=True)


def square_sums(order, rows, basis, first, n):
    tok = rows.shape[0]
    ins = [
        (rows, spec((tok, BLK), lambda i, t, w: (0, first + i))),
        (basis, spec((1, BLK, BLK), lambda i, t, w: (first + i, 0, 0))),
    ]
    out = ((n, 1, BLK), spec((1, 1, BLK), lambda i, t, w: (i, 0, 0)))
    return order(sums_body, n, ins, [out], vmem=SMALL)[0]


def total_body(table, where, *refs):
    value = (refs[0][...] + refs[1][...]) + (refs[2][...] + refs[3][...])
    refs[4][...] = value[:ROWS_C]
    if len(refs) == 6:
        refs[5][...] = value[ROWS_C:]


def total(order, parts):
    rows = parts[0].shape[0]
    outs = [full(ROWS_C, BLK)] + ([full(EXTRA, BLK)] if rows > ROWS_C else [])
    return order(total_body, 1, [(p, whole(p)) for p in parts], outs)


def mine(w):
    return w[0] * 8 + (1 - w[1]) * 4 + w[2]


def bases_body(table, where, basis_in, basis_out, *outs):
    outs[0][...], outs[1][...] = split(basis_in[0])
    outs[2][...], outs[3][...] = split(basis_out[0])


def bases(order, eig_in, eig_out):
    ins = [
        (eig_in, spec((1, BLK, BLK), lambda i, t, w: (t[mine(w)] >> 2, 0, 0))),
        (eig_out, spec((1, BLK, BLK), lambda i, t, w: (t[mine(w)] & 3, 0, 0))),
    ]
    outs = [(*full(BLK, BLK), jnp.bfloat16)] * 4
    made = order(bases_body, 1, ins, outs)
    return made[:2], made[2:]


def rotate_body(table, where, high, low, *refs):
    parts, out = refs[:-1], refs[-1]
    value = parts[0][...] + parts[1][...]
    if len(parts) > 2:
        value = value + (parts[2][...] + parts[3][...])
        value = jnp.concatenate([value, parts[4][...]], axis=0)
    out[...] = dot3(split(value), (high[...], low[...]), ((1,), (0,)))


def rotate(order, basis, parts):
    ins = [(a, whole(a)) for a in (*basis, *parts)]
    rows = parts[0].shape[0] * (1 if len(parts) == 2 else 2)
    return order(rotate_body, 1, ins, [full(rows, BLK)])[0]


def precondition_body(tokens_all, table, where, *refs):
    x, c, y0, y1, ours, theirs = (r[...] for r in refs[:6])
    a, b = (refs[6][...], refs[7][...]), (refs[8][...], refs[9][...])
    out = refs[10]
    scale = 1.0 / tokens_all
    values_in = (ours[0:1] + theirs[2:3]) * scale
    values_out = (ours[1:2] + theirs[3:4]) * scale
    y = dot3(split(y0 + y1), a, ((1,), (0,)))
    rotated = jnp.concatenate([x, y, c], axis=0) * scale
    rotated = dot3(b, split(rotated), ((0,), (0,)))
    scaled = rotated / (values_out.reshape(BLK, 1) * values_in + DAMPING)
    back = dot3(b, split(scaled), ((1,), (0,)))
    out[...] = dot3(a, split(back), ((1,), (1,)))


def precondition(tokens_all, order, parts, basis_in, basis_out):
    ins = [(q, whole(q)) for q in (*parts, *basis_in, *basis_out)]
    return order(
        functools.partial(precondition_body, tokens_all),
        1,
        ins,
        [full(BLK, BLK)],
        vmem=TURN,
    )[0]


def on_device(latents, out_grads, eig_in, eig_out, table):
    tokens_all = latents.shape[0] * N_TM
    tm = lax.axis_index("tm")
    fsdp = lax.axis_index("fsdp")
    x, zl, y = tm // 8, (tm // 4) % 2, tm % 4
    zh, core = fsdp // 2, fsdp % 2
    where = jnp.stack([x, zl, y]).astype(jnp.int32)
    near, cross = pairs_z(1), pairs_z(-1)
    send = lambda value, pairs: lax.ppermute(value, AXES, pairs)
    hop = lambda value, axis, d: send(value, pairs_far(axis, d))
    both = lambda forth, back, axis: [hop(forth, axis, 1), hop(back, axis, 3)]
    order = Order(table, where)
    far = lambda parts, axis: [parts[0]] + [hop(parts[d], axis, d) for d in (1, 2, 3)]

    turned, *sets_a = first_products(order, latents, out_grads)
    got_a = both(*sets_a[:2], "x") + both(*sets_a[2:], "y")
    got_c = send(products(order, turned, latents, SETS_AWAY)[0], near)
    made = products(order, turned, latents, SETS_B + SETS_T)
    got_b = both(*made[:2], "x") + both(*made[2:4], "y")
    sets_t = relay(order, got_a, made[4:])
    sums = [square_sums(order, latents, eig_in, 0, 4)]
    basis_in, basis_out = bases(order, eig_in, eig_out)
    got_t = both(*order.gate(sets_t[:2], got_b[:2]), "x")
    got_t += both(*order.gate(sets_t[2:], got_b[2:]), "y")
    got_b = [got_b[n] for n in (1, 0, 3, 2)]
    *own, terms_c = products(order, turned, latents, SETS_OWN + SETS_KEEP, got_b)
    sums.append(square_sums(order, latents, eig_in, 4, 4))
    sums.append(square_sums(order, out_grads, eig_out, 0, 4))

    halves = {
        stream: ((own[n], got_t[n]), (own[n + 1], got_t[n + 1]))
        for n, stream in ((0, "x"), (2, "y"))
    }
    rest = (halves, got_c, terms_c, sums)
    msgs_x = both(*turn(order, "x", MESSAGES, *rest), "y")
    msgs_y = both(*turn(order, "y", MESSAGES, *rest), "x")
    *parts_x, mine_x = turn(order, "x", TERMS, *rest)
    *parts_y, mine_y = turn(order, "y", TERMS, *rest)

    def follow(stream, messages, parts):
        more = [relay_half(order, m, p) for m, p in zip(messages, parts)]
        return both(*more, "y" if stream == "x" else "x")

    more_x = follow("x", msgs_x, parts_x)
    more_y = follow("y", msgs_y, parts_y)

    away_x, keep_x, *parts_cy = end(order, "x", mine_x, *msgs_x, *more_x)
    got_x = send(away_x, near)
    parts_cy = far(parts_cy, "x")
    order.also = [parts_cy[1], parts_cy[3]]
    away_y, keep_y, *parts_cx = end(order, "y", mine_y, *msgs_y, *more_y)
    got_y = send(away_y, near)
    turned_x = rotate(order, basis_in, [keep_x, got_x])
    done_cy, ours = total(order, parts_cy)
    theirs = send(ours, near)
    turned_c = rotate(order, basis_in, [*far(parts_cx, "y"), done_cy])
    update = precondition(
        tokens_all,
        order,
        [turned_x, turned_c, keep_y, got_y, ours, theirs],
        basis_in,
        basis_out,
    )
    same = send(update, near)
    other = send(update, cross)
    same_core = send(same, pairs_core())
    other_core = send(other, pairs_core())
    result = jnp.zeros((N_FSDP, BLK, BLK), jnp.float32)
    for block, at in (
        (same, zh * 2 + core),
        (other, (1 - zh) * 2 + core),
        (same_core, zh * 2 + 1 - core),
        (other_core, (1 - zh) * 2 + 1 - core),
    ):
        result = lax.dynamic_update_index_in_dim(result, block, at, 0)
    return result[:, None]


def solution(mesh):
    in_specs = (P("tm", None), P("tm", "fsdp"), P(), P("fsdp", None, None), P())
    out_specs = P(None, "tm", None, None)
    return jax.shard_map(
        on_device, mesh=mesh, in_specs=in_specs, out_specs=out_specs, check_vma=False
    )
```

```python
import functools

import jax
import jax.numpy as jnp
from jax import lax
from jax.experimental import pallas as pl
from jax.experimental.pallas import tpu as pltpu
from jax.sharding import PartitionSpec as P

DAMPING = 0.0001
AXES = ("tm", "fsdp")
NX, NZ, NY = 4, 2, 4
N_TM, N_FSDP = 32, 4
BLK = 512
ROWS_A = 192
ROWS_C = (BLK - 2 * ROWS_A) // 2
EXTRA = 8
SMALL, TURN, LARGE = 16 * 1024 * 1024, 30 * 1024 * 1024, 56 * 1024 * 1024


def flat(x, zl, y, zh, core):
    return ((x % NX) * 8 + zl * 4 + (y % NY)) * N_FSDP + zh * 2 + core


def coords():
    for x in range(NX):
        for zl in range(NZ):
            for y in range(NY):
                for zh in range(2):
                    for core in range(2):
                        yield x, zl, y, zh, core


def pairs_far(axis, d):
    return [
        (flat(x, zl, y, zh, c), flat(x + d * (axis == "x"), zl, y + d * (axis == "y"), zh, c))
        for x, zl, y, zh, c in coords()
    ]


def pairs_z(step):
    out = []
    for x, zl, y, zh, c in coords():
        z = (zh * 2 + zl + (step if zl == 0 else -step)) % 4
        out.append((flat(x, zl, y, zh, c), flat(x, z % 2, y, z // 2, c)))
    return out


def pairs_core():
    return [
        (flat(x, zl, y, zh, c), flat(x, zl, y, zh, 1 - c))
        for x, zl, y, zh, c in coords()
    ]


def split(value):
    high = value.astype(jnp.bfloat16)
    low = (value - high.astype(jnp.float32)).astype(jnp.bfloat16)
    return high, low


def dot3(a, b, dims):
    (ah, al), (bh, bl) = a, b
    dot = functools.partial(
        lax.dot_general,
        dimension_numbers=(dims, ((), ())),
        preferred_element_type=jnp.float32,
    )
    return dot(ah, bh) + (dot(ah, bl) + dot(al, bh))


def spot(where, stream, r, sub, i):
    z = where[1] if sub == 0 else 1 - where[1]
    if stream == "x":
        return ((where[0] + r) & 3) * 8 + z * 4 + i
    if stream == "y":
        return i * 8 + z * 4 + ((where[2] + r) & 3)
    return (i >> 2) * 8 + z * 4 + (i & 3)


def spec(shape, index, **more):
    return pl.BlockSpec(shape, index, **more)


def resident(array):
    zeros = (0,) * array.ndim
    return pl.BlockSpec(array.shape, lambda *_: zeros, pipeline_mode=pl.Buffered(1))


class Order:
    def __init__(self, table, where):
        self.table, self.where, self.last = table, where, None
        self.also = []

    def gate(self, held, behind):
        anywhere = pl.BlockSpec(memory_space=pl.ANY)
        made = pl.pallas_call(
            lambda *refs: None,
            out_shape=[jax.ShapeDtypeStruct(a.shape, a.dtype) for a in held],
            in_specs=[anywhere] * (len(held) + len(behind) + 1),
            out_specs=[anywhere] * len(held),
            input_output_aliases={i: i for i in range(len(held))},
            cost_estimate=pl.CostEstimate(flops=0, bytes_accessed=1, transcendentals=0),
        )(*held, *behind, self.last)
        self.last = made[-1]
        return made

    def __call__(self, body, grid, ins, outs, cost=1.0, vmem=SMALL):
        shapes = [
            jax.ShapeDtypeStruct(o[0], o[2] if len(o) > 2 else jnp.float32) for o in outs
        ]
        inner = body
        if self.last is not None:
            after = [self.last] + self.also
            self.also = []
            ins = [(a, pl.BlockSpec(memory_space=pl.ANY)) for a in after] + ins
            inner = lambda table, where, *refs: body(table, where, *refs[len(after) :])
        made = pl.pallas_call(
            inner,
            out_shape=shapes,
            grid_spec=pltpu.PrefetchScalarGridSpec(
                num_scalar_prefetch=2,
                grid=(grid,),
                in_specs=[s for _, s in ins],
                out_specs=[o[1] for o in outs],
            ),
            cost_estimate=pl.CostEstimate(
                flops=0, bytes_accessed=int(cost * 3.69e6), transcendentals=0
            ),
            compiler_params=pltpu.CompilerParams(vmem_limit_bytes=vmem),
        )(self.table, self.where, *[a for a, _ in ins])
        self.last = made[-1]
        return made


def piece(turned, latents, block, row, rows):
    left = turned[pl.ds(pl.multiple_of((block & 3) * BLK + row, 16), rows), :]
    right = latents[:, pl.ds(pl.multiple_of((block >> 2) * BLK, BLK), BLK)]
    return jnp.dot(left, right, preferred_element_type=jnp.float32)


SETS_A = (("x", 0, 2), ("x", 1, 2), ("y", 0, 2), ("y", 1, 2))
SETS_B = (("x", 1, 1), ("x", 0, 3), ("y", 1, 1), ("y", 0, 3))
SETS_T = (("x", 0, 1), ("x", 1, 3), ("y", 0, 1), ("y", 1, 3))
SETS_OWN = (("x", 0, 0), ("x", 1, 0), ("y", 0, 0), ("y", 1, 0))
SETS_AWAY, SETS_KEEP = (("c", 0, 0),), (("c", 1, 0),)
ROW = {"x": 0, "y": ROWS_A, "c": 2 * ROWS_A}


def first_body(table, where, grads, *refs):
    rights, turned, outs = refs[:4], refs[4], refs[5:]
    i = pl.program_id(0)

    @pl.when(i == 0)
    def _():
        for c in range(grads.shape[1] // BLK):
            turned[c * BLK : (c + 1) * BLK, :] = grads[:, c * BLK : (c + 1) * BLK].T

    for right, out, (stream, sub, r) in zip(rights, outs, SETS_A):
        block = table[spot(where, stream, r, sub, i)]
        row = (block & 3) * BLK + ROW[stream]
        left = turned[pl.ds(pl.multiple_of(row, 16), ROWS_A), :]
        out[0] = jnp.dot(left, right[...], preferred_element_type=jnp.float32)


def first_products(order, latents, out_grads):
    tok, wide = out_grads.shape
    ins = [(out_grads, resident(out_grads))]
    for job in SETS_A:
        at = lambda i, t, w, job=job: (0, t[spot(w, job[0], job[2], job[1], i)] >> 2)
        ins.append((latents, spec((tok, BLK), at)))
    outs = [((wide, tok), spec((wide, tok), lambda i, t, w: (0, 0)), out_grads.dtype)]
    for _ in SETS_A:
        outs.append(((4, ROWS_A, BLK), spec((1, ROWS_A, BLK), lambda i, t, w: (i, 0, 0))))
    return order(first_body, 4, ins, outs, vmem=LARGE)


def products_body(jobs, table, where, turned, latents, *refs):
    outs, got = refs[-len(jobs) :], refs[: -len(jobs)]
    i = pl.program_id(0)
    for m, ((stream, sub, r), out) in enumerate(zip(jobs, outs)):
        n, rows = out.shape[:2]
        for u in range(n):
            at = spot(where, stream, r, sub, n * i + u)
            value = piece(turned, latents, table[at], ROW[stream], rows)
            if m < len(got):
                value = value + got[m][u]
            out[u] = value


def products(order, turned, latents, jobs, got=()):
    outs = []
    for stream, sub, r in jobs:
        n, rows = (4, ROWS_A) if stream in "xy" else (16, 2 * ROWS_C)
        outs.append(((n, rows, BLK), spec((n // 4, rows, BLK), lambda i, t, w: (i, 0, 0))))
    return order(
        functools.partial(products_body, jobs),
        4,
        [(turned, resident(turned)), (latents, resident(latents))]
        + [(g, spec((1, ROWS_A, BLK), lambda i, t, w: (i, 0, 0))) for g in got],
        outs,
        vmem=LARGE,
    )


def whole(array):
    zeros = (0,) * array.ndim
    return spec(array.shape, lambda i, t, w: zeros)


def full(*shape):
    zeros = (0,) * len(shape)
    return (shape, spec(shape, lambda i, t, w: zeros))


def relay_body(table, where, *refs):
    for got, term, out in zip(refs[:4], refs[4:8], refs[8:]):
        out[...] = got[...] + term[...]


def relay(order, got, terms):
    here = spec((1, ROWS_A, BLK), lambda i, t, w: (i, 0, 0))
    ins = [(a, here) for a in (*got, *terms)]
    return order(relay_body, 4, ins, [(got[0].shape, here)] * 4, vmem=LARGE)


def half_rows(stream):
    return ROWS_A + 2 * (ROWS_C + (EXTRA if stream == "x" else 0))


MESSAGES = ((2, 0, (0, 0)), (1, 1, (0, 1)), (2, 1, (1, 0)), (3, 0, (1, 1)))
TERMS = ((1, 0, (0,)), (3, 1, (1,)), (0, 0, (2, 0)), (0, 1, (2, 1)))


def sum_rows_body(table, where, first_in, second_in, sums_out, out):
    for y in range(4):
        for u in range(4):
            rows = []
            for z in (1 - where[1], where[1]):
                block = table[u * 8 + z * 4 + y]
                a = block >> 2
                rows.append(jnp.where(a < 4, first_in[a & 3], second_in[a & 3]))
                rows.append(sums_out[block & 3])
            rows.append(jnp.zeros((EXTRA - 4, BLK), jnp.float32))
            out[y, u] = jnp.concatenate(rows, axis=0)


def sum_rows(order, sums):
    ins = [(s, whole(s)) for s in sums]
    return order(sum_rows_body, 1, ins, [full(4, 4, EXTRA, BLK)])[0]


def turn_body(jobs, table, where, *refs):
    refs = list(refs)
    ins = []
    for stream, *_ in jobs:
        n = 5 if stream == "x" else 4
        ins.append(refs[:n])
        refs = refs[n:]
    outs = refs
    for (stream, r, half, place), (base, more, got, term, *sums) in zip(jobs, ins):
        out = outs[place[0]].at[place[1]] if len(place) == 2 else outs[place[0]]
        out[:ROWS_A, :] = base[0] + more[0]
        rows = (half_rows(stream) - ROWS_A) // 2
        for v in range(2):
            at = (0, v) if stream == "y" else (v, 0)
            low = ROWS_A + v * rows
            out[low : low + ROWS_C, :] = got[at] + term[at]
            if stream == "x":
                out[low + ROWS_C : low + rows, :] = sums[0][0, v]


def turn(order, streams, pieces, halves, got, terms, sums):
    once = dict(pipeline_mode=pl.Buffered(1))
    ins, jobs, outs = [], [], []
    for stream in streams:
        for r, half, place in pieces:
            jobs.append((stream, r, half, (place[0] + len(outs), *place[1:])))
            if stream == "x":
                here = lambda i, t, w, r=r: ((w[2] + r) & 3, 0, 0)
                shape = (2, 1, ROWS_C, BLK)
                side = lambda i, t, w, r=r, h=half: (h, (w[2] + r) & 3, 1, 0)
            else:
                here = lambda i, t, w, r=r: ((w[0] + r) & 3, 0, 0)
                shape = (1, 2, ROWS_C, BLK)
                side = lambda i, t, w, r=r, h=half: ((w[0] + r) & 3, h, 0, 0)
            ins += [(a, spec((1, ROWS_A, BLK), here, **once)) for a in halves[stream][half]]
            for a in (got, terms):
                ins.append((a.reshape(4, 4, 2 * ROWS_C, BLK), spec(shape, side, **once)))
            if stream == "x":
                at = lambda i, t, w, r=r, h=half: ((w[2] + r) & 3, h, 0, 0)
                ins.append((sums, spec((1, 2, EXTRA, BLK), at, **once)))
        rows = half_rows(stream)
        if pieces is TERMS:
            outs += [full(rows, BLK)] * 2 + [full(2, rows, BLK)]
        else:
            outs += [full(2, rows, BLK)] * 2
    return order(functools.partial(turn_body, jobs), 1, ins, outs, vmem=TURN)


def relay_half_body(table, where, message, term, out):
    out[...] = message[0] + term[...]


def relay_half(order, message, term):
    rows = message.shape[1]
    ins = [(message, spec((1, rows, BLK), lambda i, t, w: (0, 0, 0))), (term, whole(term))]
    return order(relay_half_body, 1, ins, [full(rows, BLK)])[0]


def end_body(stream, table, where, own, forth, back, more_forth, more_back, *outs):
    halves = (
        lambda a, b: own[0, a:b] + back[1, a:b] + more_forth[a:b, :],
        lambda a, b: own[1, a:b] + forth[1, a:b] + more_back[a:b, :],
    )
    outs[0][...] = halves[0](0, ROWS_A)
    outs[1][...] = halves[1](0, ROWS_A)
    rows = (half_rows(stream) - ROWS_A) // 2
    for u in range(4):
        base = ROWS_A + (u % 2) * rows
        slot = halves[u // 2](base, base + rows)
        for d in range(4):

            @pl.when(((where[0 if stream == "x" else 2] + d) & 3) == u)
            def _():
                outs[2 + d][...] = slot


def end(order, stream, own, forth, back, more_forth, more_back):
    rows = (half_rows(stream) - ROWS_A) // 2
    outs = [full(ROWS_A, BLK)] * 2 + [full(rows, BLK)] * 4
    ins = [(a, whole(a)) for a in (own, forth, back, more_forth, more_back)]
    return order(functools.partial(end_body, stream), 1, ins, outs)


def sums_body(table, where, rows, basis, out):
    high, low = split(basis[0])
    tokens = rows[...]
    moved = jnp.dot(
        jnp.concatenate([tokens, tokens], axis=1),
        jnp.concatenate([high, low], axis=0),
        preferred_element_type=jnp.float32,
    )
    out[0] = jnp.sum(moved * moved, axis=0, keepdims=True)


def square_sums(order, rows, basis, first, n):
    tok = rows.shape[0]
    ins = [
        (rows, spec((tok, BLK), lambda i, t, w: (0, first + i))),
        (basis, spec((1, BLK, BLK), lambda i, t, w: (first + i, 0, 0))),
    ]
    out = ((n, 1, BLK), spec((1, 1, BLK), lambda i, t, w: (i, 0, 0)))
    return order(sums_body, n, ins, [out], vmem=SMALL)[0]


def total_body(table, where, *refs):
    value = (refs[0][...] + refs[1][...]) + (refs[2][...] + refs[3][...])
    refs[4][...] = value[:ROWS_C]
    if len(refs) == 6:
        refs[5][...] = value[ROWS_C:]


def total(order, parts):
    rows = parts[0].shape[0]
    outs = [full(ROWS_C, BLK)] + ([full(EXTRA, BLK)] if rows > ROWS_C else [])
    return order(total_body, 1, [(p, whole(p)) for p in parts], outs)


def mine(w):
    return w[0] * 8 + (1 - w[1]) * 4 + w[2]


def bases_body(table, where, basis_in, basis_out, *outs):
    outs[0][...], outs[1][...] = split(basis_in[0])
    outs[2][...], outs[3][...] = split(basis_out[0])


def bases(order, eig_in, eig_out):
    ins = [
        (eig_in, spec((1, BLK, BLK), lambda i, t, w: (t[mine(w)] >> 2, 0, 0))),
        (eig_out, spec((1, BLK, BLK), lambda i, t, w: (t[mine(w)] & 3, 0, 0))),
    ]
    outs = [(*full(BLK, BLK), jnp.bfloat16)] * 4
    made = order(bases_body, 1, ins, outs)
    return made[:2], made[2:]


def rotate_body(table, where, high, low, *refs):
    parts, out = refs[:-1], refs[-1]
    value = parts[0][...] + parts[1][...]
    if len(parts) > 2:
        value = value + (parts[2][...] + parts[3][...])
        value = jnp.concatenate([value, parts[4][...]], axis=0)
    out[...] = dot3(split(value), (high[...], low[...]), ((1,), (0,)))


def rotate(order, basis, parts):
    ins = [(a, whole(a)) for a in (*basis, *parts)]
    rows = parts[0].shape[0] * (1 if len(parts) == 2 else 2)
    return order(rotate_body, 1, ins, [full(rows, BLK)])[0]


def precondition_body(tokens_all, table, where, *refs):
    x, c, y0, y1, ours, theirs = (r[...] for r in refs[:6])
    a, b = (refs[6][...], refs[7][...]), (refs[8][...], refs[9][...])
    out = refs[10]
    scale = 1.0 / tokens_all
    values_in = (ours[0:1] + theirs[2:3]) * scale
    values_out = (ours[1:2] + theirs[3:4]) * scale
    y = dot3(split(y0 + y1), a, ((1,), (0,)))
    rotated = jnp.concatenate([x, y, c], axis=0) * scale
    rotated = dot3(b, split(rotated), ((0,), (0,)))
    scaled = rotated / (values_out.reshape(BLK, 1) * values_in + DAMPING)
    back = dot3(b, split(scaled), ((1,), (0,)))
    out[...] = dot3(a, split(back), ((1,), (1,)))


def precondition(tokens_all, order, parts, basis_in, basis_out):
    ins = [(q, whole(q)) for q in (*parts, *basis_in, *basis_out)]
    return order(
        functools.partial(precondition_body, tokens_all),
        1,
        ins,
        [full(BLK, BLK)],
        vmem=TURN,
    )[0]


def on_device(latents, out_grads, eig_in, eig_out, table):
    tokens_all = latents.shape[0] * N_TM
    tm = lax.axis_index("tm")
    fsdp = lax.axis_index("fsdp")
    x, zl, y = tm // 8, (tm // 4) % 2, tm % 4
    zh, core = fsdp // 2, fsdp % 2
    where = jnp.stack([x, zl, y]).astype(jnp.int32)
    near, cross = pairs_z(1), pairs_z(-1)
    send = lambda value, pairs: lax.ppermute(value, AXES, pairs)
    hop = lambda value, axis, d: send(value, pairs_far(axis, d))
    both = lambda forth, back, axis: [hop(forth, axis, 1), hop(back, axis, 3)]
    order = Order(table, where)
    far = lambda parts, axis: [parts[0]] + [hop(parts[d], axis, d) for d in (1, 2, 3)]

    turned, *sets_a = first_products(order, latents, out_grads)
    got_a = both(*sets_a[:2], "x") + both(*sets_a[2:], "y")
    got_c = send(products(order, turned, latents, SETS_AWAY)[0], near)
    made = products(order, turned, latents, SETS_B + SETS_T)
    got_b = both(*made[:2], "x") + both(*made[2:4], "y")
    sets_t = relay(order, got_a, made[4:])
    sums = [
        square_sums(order, latents, eig_in, 0, 4),
        square_sums(order, latents, eig_in, 4, 4),
    ]
    basis_in, basis_out = bases(order, eig_in, eig_out)
    got_t = both(*order.gate(sets_t[:2], got_b[:2]), "x")
    got_t += both(*order.gate(sets_t[2:], got_b[2:]), "y")
    got_b = [got_b[n] for n in (1, 0, 3, 2)]
    *own, terms_c = products(order, turned, latents, SETS_OWN + SETS_KEEP, got_b)
    sums.append(square_sums(order, out_grads, eig_out, 0, 4))
    sums = sum_rows(order, sums)

    halves = {
        stream: ((own[n], got_t[n]), (own[n + 1], got_t[n + 1]))
        for n, stream in ((0, "x"), (2, "y"))
    }
    rest = (halves, got_c, terms_c, sums)
    msgs_x = both(*turn(order, "x", MESSAGES, *rest), "y")
    msgs_y = both(*turn(order, "y", MESSAGES, *rest), "x")
    *parts_x, mine_x = turn(order, "x", TERMS, *rest)
    *parts_y, mine_y = turn(order, "y", TERMS, *rest)

    def follow(stream, messages, parts):
        more = [relay_half(order, m, p) for m, p in zip(messages, parts)]
        return both(*more, "y" if stream == "x" else "x")

    more_x = follow("x", msgs_x, parts_x)
    more_y = follow("y", msgs_y, parts_y)

    away_x, keep_x, *parts_cy = end(order, "x", mine_x, *msgs_x, *more_x)
    got_x = send(away_x, near)
    parts_cy = far(parts_cy, "x")
    order.also = [parts_cy[1], parts_cy[3]]
    away_y, keep_y, *parts_cx = end(order, "y", mine_y, *msgs_y, *more_y)
    got_y = send(away_y, near)
    turned_x = rotate(order, basis_in, [keep_x, got_x])
    done_cy, ours = total(order, parts_cy)
    theirs = send(ours, near)
    turned_c = rotate(order, basis_in, [*far(parts_cx, "y"), done_cy])
    update = precondition(
        tokens_all,
        order,
        [turned_x, turned_c, keep_y, got_y, ours, theirs],
        basis_in,
        basis_out,
    )
    same = send(update, near)
    other = send(update, cross)
    same_core = send(same, pairs_core())
    other_core = send(other, pairs_core())
    result = jnp.zeros((N_FSDP, BLK, BLK), jnp.float32)
    for block, at in (
        (same, zh * 2 + core),
        (other, (1 - zh) * 2 + core),
        (same_core, zh * 2 + 1 - core),
        (other_core, (1 - zh) * 2 + 1 - core),
    ):
        result = lax.dynamic_update_index_in_dim(result, block, at, 0)
    return result[:, None]


def solution(mesh):
    in_specs = (P("tm", None), P("tm", "fsdp"), P(), P("fsdp", None, None), P())
    out_specs = P(None, "tm", None, None)
    return jax.shard_map(
        on_device, mesh=mesh, in_specs=in_specs, out_specs=out_specs, check_vma=False
    )
```

```python
import functools

import jax
import jax.numpy as jnp
from jax import lax
from jax.experimental import pallas as pl
from jax.experimental.pallas import tpu as pltpu
from jax.sharding import PartitionSpec as P

DAMPING = 0.0001
AXES = ("tm", "fsdp")
NX, NZ, NY = 4, 2, 4
N_TM, N_FSDP = 32, 4
BLK = 512
ROWS_A = 192
ROWS_C = (BLK - 2 * ROWS_A) // 2
EXTRA = 8
SMALL, TURN, LARGE = 16 * 1024 * 1024, 30 * 1024 * 1024, 56 * 1024 * 1024


def flat(x, zl, y, zh, core):
    return ((x % NX) * 8 + zl * 4 + (y % NY)) * N_FSDP + zh * 2 + core


def coords():
    for x in range(NX):
        for zl in range(NZ):
            for y in range(NY):
                for zh in range(2):
                    for core in range(2):
                        yield x, zl, y, zh, core


def pairs_far(axis, d):
    return [
        (flat(x, zl, y, zh, c), flat(x + d * (axis == "x"), zl, y + d * (axis == "y"), zh, c))
        for x, zl, y, zh, c in coords()
    ]


def pairs_z(step):
    out = []
    for x, zl, y, zh, c in coords():
        z = (zh * 2 + zl + (step if zl == 0 else -step)) % 4
        out.append((flat(x, zl, y, zh, c), flat(x, z % 2, y, z // 2, c)))
    return out


def pairs_core():
    return [
        (flat(x, zl, y, zh, c), flat(x, zl, y, zh, 1 - c))
        for x, zl, y, zh, c in coords()
    ]


def split(value):
    high = value.astype(jnp.bfloat16)
    low = (value - high.astype(jnp.float32)).astype(jnp.bfloat16)
    return high, low


def dot3(a, b, dims):
    (ah, al), (bh, bl) = a, b
    dot = functools.partial(
        lax.dot_general,
        dimension_numbers=(dims, ((), ())),
        preferred_element_type=jnp.float32,
    )
    return dot(ah, bh) + (dot(ah, bl) + dot(al, bh))


def spot(where, stream, r, sub, i):
    z = where[1] if sub == 0 else 1 - where[1]
    if stream == "x":
        return ((where[0] + r) & 3) * 8 + z * 4 + i
    if stream == "y":
        return i * 8 + z * 4 + ((where[2] + r) & 3)
    return (i >> 2) * 8 + z * 4 + (i & 3)


def spec(shape, index, **more):
    return pl.BlockSpec(shape, index, **more)


def resident(array):
    zeros = (0,) * array.ndim
    return pl.BlockSpec(array.shape, lambda *_: zeros, pipeline_mode=pl.Buffered(1))


class Order:
    def __init__(self, table, where):
        self.table, self.where, self.last = table, where, None
        self.also = []

    def gate(self, held, behind):
        anywhere = pl.BlockSpec(memory_space=pl.ANY)
        made = pl.pallas_call(
            lambda *refs: None,
            out_shape=[jax.ShapeDtypeStruct(a.shape, a.dtype) for a in held],
            in_specs=[anywhere] * (len(held) + len(behind) + 1),
            out_specs=[anywhere] * len(held),
            input_output_aliases={i: i for i in range(len(held))},
            cost_estimate=pl.CostEstimate(flops=0, bytes_accessed=1, transcendentals=0),
        )(*held, *behind, self.last)
        self.last = made[-1]
        return made

    def __call__(self, body, grid, ins, outs, cost=1.0, vmem=SMALL):
        shapes = [
            jax.ShapeDtypeStruct(o[0], o[2] if len(o) > 2 else jnp.float32) for o in outs
        ]
        inner = body
        if self.last is not None:
            after = [self.last] + self.also
            self.also = []
            ins = [(a, pl.BlockSpec(memory_space=pl.ANY)) for a in after] + ins
            inner = lambda table, where, *refs: body(table, where, *refs[len(after) :])
        made = pl.pallas_call(
            inner,
            out_shape=shapes,
            grid_spec=pltpu.PrefetchScalarGridSpec(
                num_scalar_prefetch=2,
                grid=(grid,),
                in_specs=[s for _, s in ins],
                out_specs=[o[1] for o in outs],
            ),
            cost_estimate=pl.CostEstimate(
                flops=0, bytes_accessed=int(cost * 3.69e6), transcendentals=0
            ),
            compiler_params=pltpu.CompilerParams(vmem_limit_bytes=vmem),
        )(self.table, self.where, *[a for a, _ in ins])
        self.last = made[-1]
        return made


def piece(turned, latents, block, row, rows):
    left = turned[pl.ds(pl.multiple_of((block & 3) * BLK + row, 16), rows), :]
    right = latents[:, pl.ds(pl.multiple_of((block >> 2) * BLK, BLK), BLK)]
    return jnp.dot(left, right, preferred_element_type=jnp.float32)


SETS_A = (("x", 0, 2), ("x", 1, 2), ("y", 0, 2), ("y", 1, 2))
SETS_B = (("x", 1, 1), ("x", 0, 3), ("y", 1, 1), ("y", 0, 3))
SETS_T = (("x", 0, 1), ("x", 1, 3), ("y", 0, 1), ("y", 1, 3))
SETS_OWN = (("x", 0, 0), ("x", 1, 0), ("y", 0, 0), ("y", 1, 0))
SETS_AWAY, SETS_KEEP = (("c", 0, 0),), (("c", 1, 0),)
ROW = {"x": 0, "y": ROWS_A, "c": 2 * ROWS_A}


def first_body(table, where, grads, *refs):
    rights, turned, outs = refs[:4], refs[4], refs[5:]
    i = pl.program_id(0)

    @pl.when(i == 0)
    def _():
        for c in range(grads.shape[1] // BLK):
            turned[c * BLK : (c + 1) * BLK, :] = grads[:, c * BLK : (c + 1) * BLK].T

    for right, out, (stream, sub, r) in zip(rights, outs, SETS_A):
        block = table[spot(where, stream, r, sub, i)]
        row = (block & 3) * BLK + ROW[stream]
        left = turned[pl.ds(pl.multiple_of(row, 16), ROWS_A), :]
        out[0] = jnp.dot(left, right[...], preferred_element_type=jnp.float32)


def first_products(order, latents, out_grads):
    tok, wide = out_grads.shape
    ins = [(out_grads, resident(out_grads))]
    for job in SETS_A:
        at = lambda i, t, w, job=job: (0, t[spot(w, job[0], job[2], job[1], i)] >> 2)
        ins.append((latents, spec((tok, BLK), at)))
    outs = [((wide, tok), spec((wide, tok), lambda i, t, w: (0, 0)), out_grads.dtype)]
    for _ in SETS_A:
        outs.append(((4, ROWS_A, BLK), spec((1, ROWS_A, BLK), lambda i, t, w: (i, 0, 0))))
    return order(first_body, 4, ins, outs, vmem=LARGE)


def products_body(jobs, table, where, turned, latents, *refs):
    outs, got = refs[-len(jobs) :], refs[: -len(jobs)]
    i = pl.program_id(0)
    for m, ((stream, sub, r), out) in enumerate(zip(jobs, outs)):
        n, rows = out.shape[:2]
        for u in range(n):
            at = spot(where, stream, r, sub, n * i + u)
            value = piece(turned, latents, table[at], ROW[stream], rows)
            if m < len(got):
                value = value + got[m][u]
            out[u] = value


def products(order, turned, latents, jobs, got=()):
    outs = []
    for stream, sub, r in jobs:
        n, rows = (4, ROWS_A) if stream in "xy" else (16, 2 * ROWS_C)
        outs.append(((n, rows, BLK), spec((n // 4, rows, BLK), lambda i, t, w: (i, 0, 0))))
    return order(
        functools.partial(products_body, jobs),
        4,
        [(turned, resident(turned)), (latents, resident(latents))]
        + [(g, spec((1, ROWS_A, BLK), lambda i, t, w: (i, 0, 0))) for g in got],
        outs,
        vmem=LARGE,
    )


def whole(array):
    zeros = (0,) * array.ndim
    return spec(array.shape, lambda i, t, w: zeros)


def full(*shape):
    zeros = (0,) * len(shape)
    return (shape, spec(shape, lambda i, t, w: zeros))


def relay_body(table, where, *refs):
    for got, term, out in zip(refs[:4], refs[4:8], refs[8:]):
        out[...] = got[...] + term[...]


def relay(order, got, terms):
    here = spec((1, ROWS_A, BLK), lambda i, t, w: (i, 0, 0))
    ins = [(a, here) for a in (*got, *terms)]
    return order(relay_body, 4, ins, [(got[0].shape, here)] * 4, vmem=LARGE)


def half_rows(stream):
    return ROWS_A + 2 * (ROWS_C + (EXTRA if stream == "x" else 0))


MESSAGES = ((2, 0, (0, 0)), (1, 1, (0, 1)), (2, 1, (1, 0)), (3, 0, (1, 1)))
TERMS = ((1, 0, (0,)), (3, 1, (1,)), (0, 0, (2, 0)), (0, 1, (2, 1)))


def sum_rows_body(table, where, first_in, second_in, sums_out, out):
    for y in range(4):
        for u in range(4):
            rows = []
            for z in (1 - where[1], where[1]):
                block = table[u * 8 + z * 4 + y]
                a = block >> 2
                rows.append(jnp.where(a < 4, first_in[a & 3], second_in[a & 3]))
                rows.append(sums_out[block & 3])
            rows.append(jnp.zeros((EXTRA - 4, BLK), jnp.float32))
            out[y, u] = jnp.concatenate(rows, axis=0)


def sum_rows(order, sums):
    ins = [(s, whole(s)) for s in sums]
    return order(sum_rows_body, 1, ins, [full(4, 4, EXTRA, BLK)])[0]


def turn_body(jobs, table, where, *refs):
    refs = list(refs)
    ins = []
    for stream, *_ in jobs:
        n = 5 if stream == "x" else 4
        ins.append(refs[:n])
        refs = refs[n:]
    outs = refs
    for (stream, r, half, place), (base, more, got, term, *sums) in zip(jobs, ins):
        out = outs[place[0]].at[place[1]] if len(place) == 2 else outs[place[0]]
        out[:ROWS_A, :] = base[0] + more[0]
        rows = (half_rows(stream) - ROWS_A) // 2
        for v in range(2):
            at = (0, v) if stream == "y" else (v, 0)
            low = ROWS_A + v * rows
            out[low : low + ROWS_C, :] = got[at] + term[at]
            if stream == "x":
                out[low + ROWS_C : low + rows, :] = sums[0][0, v]


def turn(order, streams, pieces, halves, got, terms, sums):
    once = dict(pipeline_mode=pl.Buffered(1))
    ins, jobs, outs = [], [], []
    for stream in streams:
        for r, half, place in pieces:
            jobs.append((stream, r, half, (place[0] + len(outs), *place[1:])))
            if stream == "x":
                here = lambda i, t, w, r=r: ((w[2] + r) & 3, 0, 0)
                shape = (2, 1, ROWS_C, BLK)
                side = lambda i, t, w, r=r, h=half: (h, (w[2] + r) & 3, 1, 0)
            else:
                here = lambda i, t, w, r=r: ((w[0] + r) & 3, 0, 0)
                shape = (1, 2, ROWS_C, BLK)
                side = lambda i, t, w, r=r, h=half: ((w[0] + r) & 3, h, 0, 0)
            ins += [(a, spec((1, ROWS_A, BLK), here, **once)) for a in halves[stream][half]]
            for a in (got, terms):
                ins.append((a.reshape(4, 4, 2 * ROWS_C, BLK), spec(shape, side, **once)))
            if stream == "x":
                at = lambda i, t, w, r=r, h=half: ((w[2] + r) & 3, h, 0, 0)
                ins.append((sums, spec((1, 2, EXTRA, BLK), at, **once)))
        rows = half_rows(stream)
        if pieces is TERMS:
            outs += [full(rows, BLK)] * 2 + [full(2, rows, BLK)]
        else:
            outs += [full(2, rows, BLK)] * 2
    return order(functools.partial(turn_body, jobs), 1, ins, outs, vmem=TURN)


def relay_half_body(table, where, *refs):
    for message, term, out in zip(refs[:2], refs[2:4], refs[4:]):
        out[...] = message[0] + term[...]


def relay_half(order, messages, terms):
    rows = messages[0].shape[1]
    half = spec((1, rows, BLK), lambda i, t, w: (0, 0, 0))
    ins = [(m, half) for m in messages] + [(a, whole(a)) for a in terms]
    return order(relay_half_body, 1, ins, [full(rows, BLK)] * 2)


def end_body(stream, table, where, own, forth, back, more_forth, more_back, *outs):
    halves = (
        lambda a, b: own[0, a:b] + back[1, a:b] + more_forth[a:b, :],
        lambda a, b: own[1, a:b] + forth[1, a:b] + more_back[a:b, :],
    )
    outs[0][...] = halves[0](0, ROWS_A)
    outs[1][...] = halves[1](0, ROWS_A)
    rows = (half_rows(stream) - ROWS_A) // 2
    for u in range(4):
        base = ROWS_A + (u % 2) * rows
        slot = halves[u // 2](base, base + rows)
        for d in range(4):

            @pl.when(((where[0 if stream == "x" else 2] + d) & 3) == u)
            def _():
                outs[2 + d][...] = slot


def end(order, stream, own, forth, back, more_forth, more_back):
    rows = (half_rows(stream) - ROWS_A) // 2
    outs = [full(ROWS_A, BLK)] * 2 + [full(rows, BLK)] * 4
    ins = [(a, whole(a)) for a in (own, forth, back, more_forth, more_back)]
    return order(functools.partial(end_body, stream), 1, ins, outs)


def sums_body(table, where, rows, basis, out):
    high, low = split(basis[0])
    tokens = rows[...]
    moved = jnp.dot(
        jnp.concatenate([tokens, tokens], axis=1),
        jnp.concatenate([high, low], axis=0),
        preferred_element_type=jnp.float32,
    )
    out[0] = jnp.sum(moved * moved, axis=0, keepdims=True)


def square_sums(order, rows, basis, first, n):
    tok = rows.shape[0]
    ins = [
        (rows, spec((tok, BLK), lambda i, t, w: (0, first + i))),
        (basis, spec((1, BLK, BLK), lambda i, t, w: (first + i, 0, 0))),
    ]
    out = ((n, 1, BLK), spec((1, 1, BLK), lambda i, t, w: (i, 0, 0)))
    return order(sums_body, n, ins, [out], vmem=SMALL)[0]


def total_body(table, where, *refs):
    value = (refs[0][...] + refs[1][...]) + (refs[2][...] + refs[3][...])
    refs[4][...] = value[:ROWS_C]
    if len(refs) == 6:
        refs[5][...] = value[ROWS_C:]


def total(order, parts):
    rows = parts[0].shape[0]
    outs = [full(ROWS_C, BLK)] + ([full(EXTRA, BLK)] if rows > ROWS_C else [])
    return order(total_body, 1, [(p, whole(p)) for p in parts], outs)


def mine(w):
    return w[0] * 8 + (1 - w[1]) * 4 + w[2]


def bases_body(table, where, basis_in, basis_out, *outs):
    outs[0][...], outs[1][...] = split(basis_in[0])
    outs[2][...], outs[3][...] = split(basis_out[0])


def bases(order, eig_in, eig_out):
    ins = [
        (eig_in, spec((1, BLK, BLK), lambda i, t, w: (t[mine(w)] >> 2, 0, 0))),
        (eig_out, spec((1, BLK, BLK), lambda i, t, w: (t[mine(w)] & 3, 0, 0))),
    ]
    outs = [(*full(BLK, BLK), jnp.bfloat16)] * 4
    made = order(bases_body, 1, ins, outs)
    return made[:2], made[2:]


def rotate_body(table, where, high, low, *refs):
    parts, out = refs[:-1], refs[-1]
    value = parts[0][...] + parts[1][...]
    if len(parts) > 2:
        value = value + (parts[2][...] + parts[3][...])
        value = jnp.concatenate([value, parts[4][...]], axis=0)
    out[...] = dot3(split(value), (high[...], low[...]), ((1,), (0,)))


def rotate(order, basis, parts):
    ins = [(a, whole(a)) for a in (*basis, *parts)]
    rows = parts[0].shape[0] * (1 if len(parts) == 2 else 2)
    return order(rotate_body, 1, ins, [full(rows, BLK)])[0]


def precondition_body(tokens_all, table, where, *refs):
    x, c, y0, y1, ours, theirs = (r[...] for r in refs[:6])
    a, b = (refs[6][...], refs[7][...]), (refs[8][...], refs[9][...])
    out = refs[10]
    scale = 1.0 / tokens_all
    values_in = (ours[0:1] + theirs[2:3]) * scale
    values_out = (ours[1:2] + theirs[3:4]) * scale
    y = dot3(split(y0 + y1), a, ((1,), (0,)))
    rotated = jnp.concatenate([x, y, c], axis=0) * scale
    rotated = dot3(b, split(rotated), ((0,), (0,)))
    scaled = rotated / (values_out.reshape(BLK, 1) * values_in + DAMPING)
    back = dot3(b, split(scaled), ((1,), (0,)))
    out[...] = dot3(a, split(back), ((1,), (1,)))


def precondition(tokens_all, order, parts, basis_in, basis_out):
    ins = [(q, whole(q)) for q in (*parts, *basis_in, *basis_out)]
    return order(
        functools.partial(precondition_body, tokens_all),
        1,
        ins,
        [full(BLK, BLK)],
        vmem=TURN,
    )[0]


def on_device(latents, out_grads, eig_in, eig_out, table):
    tokens_all = latents.shape[0] * N_TM
    tm = lax.axis_index("tm")
    fsdp = lax.axis_index("fsdp")
    x, zl, y = tm // 8, (tm // 4) % 2, tm % 4
    zh, core = fsdp // 2, fsdp % 2
    where = jnp.stack([x, zl, y]).astype(jnp.int32)
    near, cross = pairs_z(1), pairs_z(-1)
    send = lambda value, pairs: lax.ppermute(value, AXES, pairs)
    hop = lambda value, axis, d: send(value, pairs_far(axis, d))
    both = lambda forth, back, axis: [hop(forth, axis, 1), hop(back, axis, 3)]
    order = Order(table, where)
    far = lambda parts, axis: [parts[0]] + [hop(parts[d], axis, d) for d in (1, 2, 3)]

    turned, *sets_a = first_products(order, latents, out_grads)
    got_a = both(*sets_a[:2], "x") + both(*sets_a[2:], "y")
    got_c = send(products(order, turned, latents, SETS_AWAY)[0], near)
    made = products(order, turned, latents, SETS_B + SETS_T)
    got_b = both(*made[:2], "x") + both(*made[2:4], "y")
    sets_t = relay(order, got_a, made[4:])
    sums = [
        square_sums(order, latents, eig_in, 0, 4),
        square_sums(order, latents, eig_in, 4, 4),
    ]
    basis_in, basis_out = bases(order, eig_in, eig_out)
    got_t = both(*order.gate(sets_t[:2], got_b[:2]), "x")
    got_t += both(*order.gate(sets_t[2:], got_b[2:]), "y")
    got_b = [got_b[n] for n in (1, 0, 3, 2)]
    *own, terms_c = products(order, turned, latents, SETS_OWN + SETS_KEEP, got_b)
    sums.append(square_sums(order, out_grads, eig_out, 0, 4))
    sums = sum_rows(order, sums)

    halves = {
        stream: ((own[n], got_t[n]), (own[n + 1], got_t[n + 1]))
        for n, stream in ((0, "x"), (2, "y"))
    }
    rest = (halves, got_c, terms_c, sums)
    msgs_x = both(*turn(order, "x", MESSAGES, *rest), "y")
    msgs_y = both(*turn(order, "y", MESSAGES, *rest), "x")
    *parts_x, mine_x = turn(order, "x", TERMS, *rest)
    *parts_y, mine_y = turn(order, "y", TERMS, *rest)

    def follow(stream, messages, parts):
        more = relay_half(order, messages, parts)
        return both(*more, "y" if stream == "x" else "x")

    more_x = follow("x", msgs_x, parts_x)
    more_y = follow("y", msgs_y, parts_y)

    away_x, keep_x, *parts_cy = end(order, "x", mine_x, *msgs_x, *more_x)
    got_x = send(away_x, near)
    parts_cy = far(parts_cy, "x")
    order.also = [parts_cy[1], parts_cy[3]]
    away_y, keep_y, *parts_cx = end(order, "y", mine_y, *msgs_y, *more_y)
    got_y = send(away_y, near)
    turned_x = rotate(order, basis_in, [keep_x, got_x])
    done_cy, ours = total(order, parts_cy)
    theirs = send(ours, near)
    turned_c = rotate(order, basis_in, [*far(parts_cx, "y"), done_cy])
    update = precondition(
        tokens_all,
        order,
        [turned_x, turned_c, keep_y, got_y, ours, theirs],
        basis_in,
        basis_out,
    )
    same = send(update, near)
    other = send(update, cross)
    same_core = send(same, pairs_core())
    other_core = send(other, pairs_core())
    result = jnp.zeros((N_FSDP, BLK, BLK), jnp.float32)
    for block, at in (
        (same, zh * 2 + core),
        (other, (1 - zh) * 2 + core),
        (same_core, zh * 2 + 1 - core),
        (other_core, (1 - zh) * 2 + 1 - core),
    ):
        result = lax.dynamic_update_index_in_dim(result, block, at, 0)
    return result[:, None]


def solution(mesh):
    in_specs = (P("tm", None), P("tm", "fsdp"), P(), P("fsdp", None, None), P())
    out_specs = P(None, "tm", None, None)
    return jax.shard_map(
        on_device, mesh=mesh, in_specs=in_specs, out_specs=out_specs, check_vma=False
    )
```
